128 devices in a mesh: ctx: 16 (over x, z_lo, core), vocab: 8 (over y, z_hi).
Axes of the slice: x: 4, y: 4, z: 4 (z_hi: 2, z_lo: 2; z = z_hi * 2 + z_lo), core: 2. Of those that a mesh axis runs over, the one named last changes fastest.
Arguments:
- hidden: bfloat16 [2048, 6144], P('ctx'), may hold values from -16 to 16
- labels: int32 [2048], P('ctx'), may hold values from 0 to 65535
- head_weight: bfloat16 [6144, 65536], P(None, ('ctx', 'vocab')), may hold values from -0.31894398 to 0.31894398
Outputs:
- token_loss: float32 [2048], P('ctx')
- head_grad: float32 [6144, 65536], P(None, ('ctx', 'vocab'))
The draws below stay inside these ranges and needn't reach their ends.
All inputs are finite; a program needn't handle non-finite values.
Results may differ from the reference program's by a relative error of at most 0.0021.
Values may be sent and summed in bfloat16 or wider, within the bound.
A program may use at most 128 MiB of HBM per device.

```python
import math
import jax
import jax.numpy as jnp
import numpy as np
from jax import lax

D = 6144
TOKENS = 2048
VOCAB = 65536


def draw_hidden(key, part):
    key = jax.random.fold_in(key, 1)
    noise_key, scale_key = jax.random.split(key, 2)
    raw_values = jnp.clip(jax.random.normal(noise_key, (TOKENS, D), jnp.float32), -4.0, 4.0)
    row_scale = jnp.exp(jax.random.uniform(scale_key, (TOKENS, 1), jnp.float32, math.log(0.4), math.log(4.0)))
    values = raw_values * row_scale
    return values.astype(jnp.bfloat16)


def draw_head_weight(key, part):
    key = jax.random.fold_in(key, 2)
    noise_key, scale_key = jax.random.split(key, 2)
    raw_values = jnp.clip(jax.random.normal(noise_key, (D, VOCAB), jnp.float32), -4.0, 4.0)
    col_scale = 1.5 * jnp.exp(jax.random.uniform(scale_key, (1, VOCAB), jnp.float32, math.log(0.4), math.log(4.0)))
    values = raw_values * col_scale * D ** (-0.5)
    return values.astype(jnp.bfloat16)


def set_ends(drawn, key, least, top_value):
    dims = drawn.shape
    spot = [jax.random.randint(jax.random.fold_in(key, axis), (), 0, dims[axis]) for axis in range(len(dims))]
    drawn = drawn.at[tuple(spot)].set(least)
    longest = dims.index(max(dims))
    spot[longest] = (spot[longest] + 1) % dims[longest]
    return drawn.at[tuple(spot)].set(top_value)


def rank_table(count, skew):
    loads = [(1 << 20) // math.isqrt(grade ** skew) + 1 for grade in range(1, count + 1)]
    deviation = 1 + sum(loads) // (1 << 30)
    return np.cumsum(np.array([max(1, weight // deviation) for weight in loads]))


def ranked_ids(own_key, shape, count, skew):
    listing = rank_table(count, skew)
    pick = jax.random.randint(jax.random.fold_in(own_key, 1), shape, 0, int(listing[count - 1]))
    grade = jnp.searchsorted(jnp.asarray(listing, jnp.int32), pick, side="right")
    return jax.random.permutation(jax.random.fold_in(own_key, 2), count)[grade].astype(jnp.int32)


def setup_inputs(seed: int = 0) -> dict:
    key_of = jax.random.split(jax.random.key(seed), 4)
    hidden = draw_hidden(jax.random.fold_in(key_of[3], 71), 0)
    labels = set_ends(ranked_ids(key_of[1], (TOKENS,), VOCAB, 2), jax.random.fold_in(key_of[1], 3), 0, VOCAB - 1).astype(jnp.int32)
    head_weight = draw_head_weight(jax.random.fold_in(key_of[3], 71), 0)
    return dict(hidden=hidden, labels=labels, head_weight=head_weight)


z_weight = 0.0001


def reference(hidden, labels, head_weight):
    logits = jnp.dot(hidden, head_weight, preferred_element_type=jnp.float32)
    row_top = jnp.max(logits, axis=1)
    row_total = jnp.sum(jnp.exp(logits - row_top[:, None]), axis=1)
    log_partition = row_top + jnp.log(row_total)
    label_logit = jnp.take_along_axis(logits, labels.astype(jnp.int32)[:, None], axis=1)[:, 0]
    token_loss = log_partition - label_logit + z_weight * log_partition * log_partition
    softmax_rows = jnp.exp(logits - log_partition[:, None])
    one_hot = (jnp.arange(VOCAB, dtype=jnp.int32)[None, :] == labels.astype(jnp.int32)[:, None]).astype(jnp.float32)
    logit_slope = ((1.0 + 2.0 * z_weight * log_partition)[:, None] * softmax_rows - one_hot).astype(jnp.bfloat16)
    head_grad = lax.dot_general(hidden, logit_slope, (((0,), (0,)), ((), ())), preferred_element_type=jnp.float32)
    return token_loss, head_grad
```

```python
import heapq
import jax
import jax.numpy as jnp
from jax import lax
from jax.experimental import pallas as pl
from jax.experimental.pallas import tpu as pltpu
from jax.sharding import PartitionSpec as P

MESH = pl.DeviceIdType.MESH
z_weight = 0.0001

REGIONS = ("F", "F'", "C", "S'", "S")
BLOCKS = ("0", "L", "R", "2")
LINKS = ("x+", "x-", "z+", "z-", "y+", "y-")
ORDER = {"x": ("F", "F'", "C", "S'"), "z": ("F", "F'", "C"), "y": ("F", "F'")}


def region_rows(half):
    unit = half // 48
    edge, wide = 9 * unit, 10 * unit
    return dict(zip(REGIONS, (edge, wide, wide, wide, edge)))


def starts_of(rows):
    starts, at = {}, 0
    for name in REGIONS:
        starts[name] = at
        at += rows[name]
    return starts


def onward(key):
    _, block, region, part = key
    links = []
    if block[0] != "Z":
        if region != "S":
            if block == "0":
                links += ["x+", "x-"]
            if (block, part) == ("L", 0):
                links.append("x+")
            if (block, part) == ("R", 1):
                links.append("x-")
        if region in ORDER["z"]:
            links.append(("z+", "z-")[part])
        if region == "F" and block != "0":
            links.append(("y+", "y-")[part])
    elif region in ORDER["y"]:
        links.append(("y+", "y-")[part])
    return links


def landing(link, key):
    phase, block, region, part = key
    if link[0] == "x":
        block = "2" if block != "0" else ("L" if link == "x+" else "R")
    elif link[0] == "z":
        block = "Z" + block
    else:
        region = {"F": "S", "F'": "S'"}[region]
    return phase, block, region, part


def plan(halves, tasks, first):
    row_link, row_pair, hop, pair_hop, issue, ahead = 256 / 45.5e3, 256 / 500e3, 1.7, 1.0, 0.04, 3.0
    rows = [region_rows(half) for half in halves]
    now, tick = first, 0
    busy = dict.fromkeys(LINKS + ("pair",), 0.0)
    queue = {link: [] for link in LINKS}
    coming, have, steps = [], set(), []
    tasks = list(tasks)
    near = {"0": 0, "L": 1, "R": 1, "2": 2}

    def post(when, what):
        nonlocal tick
        tick += 1
        heapq.heappush(coming, (when, tick, what))

    def rank(link, key):
        return key[0], ORDER[link[0]].index(key[2]), near[key[1][-1]], key[3]

    def pump():
        nonlocal now
        for link in LINKS:
            while queue[link] and busy[link] - now < ahead:
                key = min(queue[link], key=lambda k: rank(link, k))
                queue[link].remove(key)
                steps.append(("send", link, key))
                now += issue
                busy[link] = max(busy[link], now) + rows[key[0]][key[2]] // 2 * row_link
                post(busy[link] + hop, ("piece", landing(link, key)))

    for phase in range(len(halves)):
        for region in ORDER["x"]:
            for part in (0, 1):
                key = (phase, "0", region, part)
                for link in onward(key):
                    queue[link].append(key)
    while True:
        while coming and coming[0][0] <= now:
            kind, key = heapq.heappop(coming)[2]
            if kind == "piece":
                have.add(("here", key))
                steps.append(("take", key))
                for link in onward(key):
                    queue[link].append(key)
                busy["pair"] = max(busy["pair"], now) + rows[key[0]][key[2]] // 2 * row_pair
                post(busy["pair"] + pair_hop, ("there", key))
                now += 2 * issue
            else:
                have.add((kind, key))
            pump()
        pump()
        ready = [task for task in tasks if all(need in have for need in task[2])]
        if ready:
            name, took, _, reply = ready[0]
            tasks.remove(ready[0])
            steps.append(("task", name))
            now += took
            have.add(("done", name))
            if reply:
                post(now + reply, ("reply", name))
        elif coming:
            now = max(now, coming[0][0])
        else:
            break
    assert not tasks and not any(queue.values())
    return steps, now


def head(hidden, labels, head_weight):
    tok, depth = hidden.shape
    cols = head_weight.shape[1]
    half = depth // 2
    rows = region_rows(half)
    starts = starts_of(rows)
    n_ctx, n_vocab, phases, n_x = 16, 8, 2, 4
    per_phase = n_ctx // phases
    kpiece = 1024
    n_k = half // kpiece
    w_step = 512
    n_w = depth // w_step
    w_slots = 3
    grad_step = 1024
    n_grad = depth // grad_step

    keys = []
    for phase in range(phases):
        for block in BLOCKS[1:] + tuple("Z" + b for b in BLOCKS):
            for region in REGIONS:
                keys += [(phase, block, region, part) for part in (0, 1)]
    sem_of = {key: i for i, key in enumerate(keys)}
    groups = [(phase, b, region) for phase in range(phases) for b in BLOCKS for region in REGIONS]
    group_of = {g: i for i, g in enumerate(groups)}

    tasks = [(("w", i), 0.3, (), 0) for i in range(n_w)]
    for phase in range(phases):
        tasks.append((("merge1", phase), 0.3, (("reply", ("stats", phase)),), 4.0))
        tasks.append((("merge2", phase), 0.3, (("reply", ("merge1", phase)),), 0))
        for b in BLOCKS:
            tasks.append((("slope", phase, b), 0.3, (("done", ("merge2", phase)),), 0))
    for phase in range(phases):
        for k in range(n_k):
            for b in BLOCKS:
                needs = [("done", ("w", n_w - 1))]
                for region in REGIONS:
                    if starts[region] < (k + 1) * kpiece and starts[region] + rows[region] > k * kpiece:
                        for part in (0, 1):
                            for block in ((b, "Z" + b) if b != "0" else ("Z0",)):
                                key = (phase, block, region, part)
                                needs += [("here", key), ("there", key)]
                tasks.append((("logits", phase, k, b), 0.65, tuple(needs), 0))
        tasks.append((
            ("stats", phase), 1.0,
            tuple(("done", ("logits", phase, k, b)) for k in range(n_k) for b in BLOCKS), 5.0,
        ))
    for phase in range(phases):
        for i in range(n_grad):
            tasks.append((
                ("grad", phase, i), 1.5, tuple(("done", ("slope", phase, b)) for b in BLOCKS), 0,
            ))
    steps, _ = plan([half] * phases, tasks, 0.0)

    def kernel(hid_hbm, lab_ref, w_hbm, grad, loss, hid, H, wst, WT, LT, ST, LB, S1, S2, LP,
               hid_sem, w_sem, recv, pair_recv, own_recv, own_recv2, send, own_send, st_send, st_recv, lb_send, lb_recv):
        ctx, voc = lax.axis_index("ctx"), lax.axis_index("vocab")
        core, zl, x = ctx % 2, (ctx // 2) % 2, ctx // 4
        zh, y = voc % 2, voc // 2
        q = y % 2

        def at(xx, zz, cc):
            return (xx * 2 + zz) * 2 + cc

        own_hid = pltpu.make_async_copy(hid_hbm, hid, hid_sem)
        own_hid.start()

        def w_copy(i):
            return pltpu.make_async_copy(
                w_hbm.at[pl.ds(i * w_step, w_step), :], wst.at[i % w_slots], w_sem.at[i % w_slots])

        for i in range(w_slots):
            w_copy(i).start()

        right, left, across = (x + 1) % 4, (x + 3) % 4, (x + 2) % 4
        up, down = voc + 2, voc + 6
        zp, zm = (zh * 2 + zl + 1) % 4, (zh * 2 + zl + 3) % 4
        device = {
            "x+": (at(right, zl, core), voc),
            "x-": (at(left, zl, core), voc),
            "z+": (at(x, zp % 2, core), y * 2 + zp // 2),
            "z-": (at(x, zm % 2, core), y * 2 + zm // 2),
            "y+": (ctx, up % 8),
            "y-": (ctx, down % 8),
            "pair": (at(x, zl, 1 - core), voc),
        }
        ctx_peers = [((ctx + i) % n_ctx, voc) for i in range(1, n_ctx)]
        voc_peers = [(ctx, (voc + i) % n_vocab) for i in range(1, n_vocab)]
        cross = (at(x, 1 - zl, core), y * 2 + 1 - zh)

        barrier = pltpu.get_barrier_semaphore()
        for peer in ctx_peers + voc_peers + [cross]:
            pl.semaphore_signal(barrier, inc=1, device_id=peer, device_id_type=MESH)

        xs = {"0": x, "L": left, "R": right, "2": across}
        mine = x * 2 + zl

        def slot(phase, block):
            if block[0] == "Z":
                return phase * per_phase + xs[block[1]] * 2 + 1 - zl
            return phase * per_phase + xs[block] * 2 + zl

        def region_at(region, which):
            ahead = starts[region]
            back = half - starts[region] - rows[region]
            return which * half + jnp.where(q == 0, ahead, back)

        begin = {region: region_at(region, core) for region in REGIONS}
        begin_pair = {region: region_at(region, 1 - core) for region in REGIONS}

        def piece(key):
            phase, block, region, part = key
            n = rows[region] // 2
            return H.at[slot(phase, block), pl.ds(pl.multiple_of(begin[region] + part * n, 16), n), :]

        def link_copy(link, key):
            ref = piece(key)
            i = LINKS.index(link)
            return pltpu.make_async_remote_copy(
                src_ref=ref, dst_ref=ref, send_sem=send.at[key[0], i], recv_sem=recv.at[sem_of[landing(link, key)]],
                device_id=device[link], device_id_type=MESH)

        def take(key):
            ref = piece(key)
            pltpu.make_async_remote_copy(
                src_ref=ref, dst_ref=ref, send_sem=send.at[0, 0], recv_sem=recv.at[sem_of[key]],
                device_id=device["pair"], device_id_type=MESH).wait_recv()
            phase, block, region, _ = key
            pltpu.make_async_remote_copy(
                src_ref=ref, dst_ref=ref, send_sem=send.at[phase, 6],
                recv_sem=pair_recv.at[group_of[(phase, block[-1], region)]],
                device_id=device["pair"], device_id_type=MESH).start()

        def drain(n_rows, sem):
            full, rest = divmod(n_rows, depth)
            assert full == 0 or rest == 0
            ref = H.at[0, pl.ds(0, n_rows), :] if full == 0 else H.at[pl.ds(0, full)]
            return pltpu.make_async_remote_copy(
                src_ref=ref, dst_ref=ref, send_sem=sem, recv_sem=sem, device_id=device["pair"], device_id_type=MESH)

        own_hid.wait()
        own_slot = core * per_phase + mine
        for i in range(depth // 1024):
            H[own_slot, pl.ds(i * 1024, 1024), :] = hid[:, pl.ds(i * 1024, 1024)].T
        LB[ctx] = lab_ref[...]
        pl.semaphore_wait(barrier, len(ctx_peers) + len(voc_peers) + 1)

        def own_copy(region, theirs):
            first = (begin_pair if theirs else begin)[region]
            ref = H.at[own_slot, pl.ds(pl.multiple_of(first, 16), rows[region]), :]
            sem = own_recv.at[REGIONS.index(region)] if theirs else own_recv2
            return pltpu.make_async_remote_copy(
                src_ref=ref, dst_ref=ref, send_sem=own_send, recv_sem=sem,
                device_id=device["pair"], device_id_type=MESH)

        for region in REGIONS:
            own_copy(region, True).start()

        def own_wait(region, phase):
            @pl.when(core != phase)
            def _():
                ref = H.at[phase * per_phase + mine, pl.ds(pl.multiple_of(begin[region], 16), rows[region]), :]
                pltpu.make_async_remote_copy(
                    src_ref=ref, dst_ref=ref, send_sem=own_send, recv_sem=own_recv.at[REGIONS.index(region)],
                    device_id=device["pair"], device_id_type=MESH).wait_recv()

        own_seen, rest_sent, rest_seen, groups_seen = set(), [False], set(), set()

        def send_rest():
            for region in REGIONS:
                own_copy(region, False).start()
            for peer in ctx_peers:
                pltpu.make_async_remote_copy(
                    src_ref=LB.at[ctx], dst_ref=LB.at[ctx], send_sem=lb_send, recv_sem=lb_recv,
                    device_id=peer, device_id_type=MESH).start()

        def need_own(region, phase):
            if (region, phase) not in own_seen:
                own_seen.add((region, phase))
                own_wait(region, phase)

        def need_rest(phase):
            if phase not in rest_seen:
                rest_seen.add(phase)

                @pl.when(core != phase)
                def _():
                    drain(half, own_recv2).wait_recv()

        def need_group(phase, b, region):
            if (phase, b, region) not in groups_seen:
                groups_seen.add((phase, b, region))
                drain(rows[region] * (1 if b == "0" else 2), pair_recv.at[group_of[(phase, b, region)]]).wait_recv()

        def w_task(i):
            w_copy(i).wait()
            WT[:, pl.ds(i * w_step, w_step)] = wst[i % w_slots].T
            if i + w_slots < n_w:
                w_copy(i + w_slots).start()

        def logits_task(phase, k, b):
            for region in REGIONS:
                if starts[region] < (k + 1) * kpiece and starts[region] + rows[region] > k * kpiece:
                    need_group(phase, b, region)
                    if b == "0":
                        need_own(region, phase)
            if b == "0":
                need_rest(phase)
            xb = xs[b]
            s0 = phase * per_phase + xb * 2
            total = None
            for which in (core, 1 - core):
                off = which * half + jnp.where(q == 0, k * kpiece, half - (k + 1) * kpiece)
                off = pl.multiple_of(off, 1024)
                ks = pl.ds(off, kpiece)
                block = jnp.concatenate([H[s0, ks, :], H[s0 + 1, ks, :]], axis=1)
                part = jnp.dot(WT[:, ks], block, preferred_element_type=jnp.float32)
                total = part if total is None else total + part
            if k == 0:
                LT[phase, xb] = total
            else:
                LT[phase, xb] += total

        first_col = (ctx * n_vocab + voc) * cols
        label_seen = [False]

        def label_mask(phase, xb):
            lab = jnp.concatenate([LB[at(xb, 0, phase)], LB[at(xb, 1, phase)]], axis=1)
            ids = lax.broadcasted_iota(jnp.int32, (cols, 2 * tok), 0)
            return ids == lab - first_col

        def stats_task(phase):
            if not label_seen[0]:
                label_seen[0] = True
                pltpu.make_async_remote_copy(
                    src_ref=LB.at[pl.ds(0, n_ctx - 1)], dst_ref=LB.at[pl.ds(0, n_ctx - 1)], send_sem=lb_send,
                    recv_sem=lb_recv, device_id=device["pair"], device_id_type=MESH).wait_recv()
            for xb in range(n_x):
                lt = LT[phase, xb]
                top = jnp.max(lt, axis=0, keepdims=True)
                total = jnp.sum(jnp.exp(lt - top), axis=0, keepdims=True)
                label = jnp.sum(jnp.where(label_mask(phase, xb), lt, 0.0), axis=0, keepdims=True)
                for i, row in enumerate((top, total, label)):
                    S1[phase, ctx, i, 2 * xb:2 * xb + 1, :] = row[:, :tok]
                    S1[phase, ctx, i, 2 * xb + 1:2 * xb + 2, :] = row[:, tok:]
            for peer in ctx_peers:
                stat_copy(S1, phase, ctx, 0, peer).start()

        def stat_copy(buf, phase, index, stage, peer):
            ref = buf.at[phase, index]
            return pltpu.make_async_remote_copy(
                src_ref=ref, dst_ref=ref, send_sem=st_send.at[phase, stage], recv_sem=st_recv.at[phase, stage],
                device_id=peer, device_id_type=MESH)

        def stat_all(buf, phase, stage, n):
            ref = buf.at[phase, pl.ds(0, n - 1)]
            return pltpu.make_async_remote_copy(
                src_ref=ref, dst_ref=ref, send_sem=st_send.at[phase, stage], recv_sem=st_recv.at[phase, stage],
                device_id=device["pair"], device_id_type=MESH)

        def merged(buf, phase, n):
            tops = [buf[phase, i, 0] for i in range(n)]
            top = tops[0]
            for t in tops[1:]:
                top = jnp.maximum(top, t)
            total = sum(buf[phase, i, 1] * jnp.exp(tops[i] - top) for i in range(n))
            label = sum(buf[phase, i, 2] for i in range(n))
            return top, total, label

        def merge1_task(phase):
            stat_all(S1, phase, 0, n_ctx).wait_recv()
            for i, row in enumerate(merged(S1, phase, n_ctx)):
                S2[phase, voc, i] = row
            for peer in voc_peers:
                stat_copy(S2, phase, voc, 1, peer).start()

        def merge2_task(phase):
            stat_all(S2, phase, 1, n_vocab).wait_recv()
            top, total, label = merged(S2, phase, n_vocab)
            lp = top + jnp.log(total)
            LP[phase, 0] = lp
            LP[phase, 1] = lp - label + z_weight * lp * lp

            @pl.when(core == phase)
            def _():
                loss[...] = LP[phase, 1, pl.ds(mine, 1), :]

        def slope_task(phase, b):
            xb = BLOCKS.index(b)
            lp = jnp.concatenate([LP[phase, 0, 2 * xb:2 * xb + 1, :], LP[phase, 0, 2 * xb + 1:2 * xb + 2, :]], axis=1)
            soft = jnp.exp(LT[phase, xb] - lp)
            hot = jnp.where(label_mask(phase, xb), 1.0, 0.0)
            ST[phase, xb] = ((1.0 + 2.0 * z_weight * lp) * soft - hot).astype(jnp.bfloat16)

        def grad_task(phase, i):
            rs = pl.ds(i * grad_step, grad_step)
            lhs = jnp.concatenate([H[phase * per_phase + b, rs, :] for b in range(per_phase)], axis=1)
            rhs = jnp.concatenate([ST[phase, xb] for xb in range(n_x)], axis=1)
            part = lax.dot_general(lhs, rhs, (((1,), (1,)), ((), ())), preferred_element_type=jnp.float32)
            if phase == 0:
                grad[rs, :] = part
            else:
                grad[rs, :] += part

        run = {"w": w_task, "logits": logits_task, "stats": stats_task, "merge1": merge1_task,
               "merge2": merge2_task, "slope": slope_task, "grad": grad_task}
        for step in steps:
            if step[0] == "send":
                _, link, key = step
                if key[1] == "0":
                    need_own(key[2], key[0])
                link_copy(link, key).start()
            elif step[0] == "take":
                take(step[1])
            else:
                if not rest_sent[0]:
                    rest_sent[0] = True
                    send_rest()
                name = step[1]
                run[name[0]](*name[1:])

        for phase in range(phases):
            for i, link in enumerate(LINKS):
                n = sum(rows[s[2][2]] // 2 for s in steps if s[0] == "send" and s[1] == link and s[2][0] == phase)
                drain(n, send.at[phase, i]).wait_send()
            ref = H.at[pl.ds(0, 7), pl.ds(0, half), :]
            pltpu.make_async_remote_copy(
                src_ref=ref, dst_ref=ref, send_sem=send.at[phase, 6], recv_sem=own_recv2,
                device_id=device["pair"], device_id_type=MESH).wait_send()
            stat_all(S1, phase, 0, n_ctx).wait_send()
            stat_all(S2, phase, 1, n_vocab).wait_send()
        drain(depth, own_send).wait_send()
        pltpu.make_async_remote_copy(
            src_ref=LB.at[pl.ds(0, n_ctx - 1)], dst_ref=LB.at[pl.ds(0, n_ctx - 1)], send_sem=lb_send,
            recv_sem=lb_recv, device_id=device["pair"], device_id_type=MESH).wait_send()

    bf16, f32 = jnp.bfloat16, jnp.float32
    dma = pltpu.SemaphoreType.DMA
    grad, loss = pl.pallas_call(
        kernel,
        name="head",
        out_shape=(pltpu.VMEM((depth, cols), f32), pltpu.VMEM((1, tok), f32)),
        in_specs=[pl.BlockSpec(memory_space=pl.ANY), pl.BlockSpec(memory_space=pltpu.VMEM),
                  pl.BlockSpec(memory_space=pl.ANY)],
        out_specs=(pl.BlockSpec(memory_space=pltpu.VMEM), pl.BlockSpec(memory_space=pltpu.VMEM)),
        scratch_shapes=[
            pltpu.VMEM((tok, depth), bf16),
            pltpu.VMEM((n_ctx, depth, tok), bf16),
            pltpu.VMEM((w_slots, w_step, cols), bf16),
            pltpu.VMEM((cols, depth), bf16),
            pltpu.VMEM((phases, n_x, cols, 2 * tok), f32),
            pltpu.VMEM((phases, n_x, cols, 2 * tok), bf16),
            pltpu.VMEM((n_ctx, 1, tok), jnp.int32),
            pltpu.VMEM((phases, n_ctx, 3, per_phase, tok), f32),
            pltpu.VMEM((phases, n_vocab, 3, per_phase, tok), f32),
            pltpu.VMEM((phases, 2, per_phase, tok), f32),
            dma, dma((w_slots,)), dma((len(keys),)), dma((len(groups),)), dma((len(REGIONS),)), dma,
            dma((phases, 7)), dma, dma((phases, 2)), dma((phases, 2)), dma, dma,
        ],
        compiler_params=pltpu.CompilerParams(
            collective_id=0, has_side_effects=True, vmem_limit_bytes=48 * 2**20),
    )(hidden, labels.reshape(1, tok), head_weight)
    return loss.reshape(tok), grad


def solution(mesh):
    return jax.shard_map(
        head,
        mesh=mesh,
        in_specs=(P("ctx", None), P("ctx"), P(None, ("ctx", "vocab"))),
        out_specs=(P("ctx"), P(None, ("ctx", "vocab"))),
        check_vma=False,
    )
```

```python
import heapq
import jax
import jax.numpy as jnp
from jax import lax
from jax.experimental import pallas as pl
from jax.experimental.pallas import tpu as pltpu
from jax.sharding import PartitionSpec as P

MESH = pl.DeviceIdType.MESH
z_weight = 0.0001

TOKENS_OF = (32,64,32)
SIZES = ((4, 5, 6, 5, 4), (5, 5, 4, 5, 5), (5, 5, 4, 5, 5))
REGIONS = ("F", "F'", "C", "S'", "S")
BLOCKS = ("0", "R", "2", "L")
LINKS = ("x+", "x-", "z+", "z-", "y+", "y-")
ORDER = {"x": ("F", "F'", "C", "S'"), "z": ("F", "F'", "C"), "y": ("F", "F'")}
NEAR = {"0": 0, "L": 1, "R": 1, "2": 2}
LANES = 128
N_CTX, N_VOCAB, N_X = 16, 8, 4


def onward(key):
    _, block, region, part = key
    links = []
    if block[0] != "Z":
        if region != "S":
            if block == "0":
                links += ["x+", "x-"]
            if (block, part) == ("L", 0):
                links.append("x+")
            if (block, part) == ("R", 1):
                links.append("x-")
        if region in ORDER["z"]:
            links.append(("z+", "z-")[part])
        if region == "F" and block != "0":
            links.append(("y+", "y-")[part])
    elif region in ORDER["y"]:
        links.append(("y+", "y-")[part])
    return links


def landing(link, key):
    phase, block, region, part = key
    if link[0] == "x":
        block = "2" if block != "0" else ("L" if link == "x+" else "R")
    elif link[0] == "z":
        block = "Z" + block
    else:
        region = {"F": "S", "F'": "S'"}[region]
    return phase, block, region, part


def rank(link, key):
    return key[0], ORDER[link[0]].index(key[2]), NEAR[key[1][-1]], key[3]


def plan(toks, cols, tasks):
    link_rate, pair_rate, hop, pair_hop, issue, ahead = 43e3, 500e3, 3.0, 1.5, 0.03, 5.0
    now, tick = 0.0, 0
    busy = dict.fromkeys(LINKS + ("pair",), 0.0)
    busy["pair"] = 3.2
    queue = {link: [] for link in LINKS}
    coming, have, steps = [], set(), []
    tasks = list(tasks)

    def post(when, what):
        nonlocal tick
        tick += 1
        heapq.heappush(coming, (when, tick, what))

    def size(key):
        return 2 * toks[key[0]] * cols[key[0]][key[2]]

    def pump():
        nonlocal now
        for link in LINKS:
            while queue[link] and busy[link] - now < ahead:
                key = min(queue[link], key=lambda k: rank(link, k))
                queue[link].remove(key)
                steps.append(("send", link, key))
                now += issue
                busy[link] = max(busy[link], now) + size(key) / link_rate
                post(busy[link] + hop, ("piece", landing(link, key)))

    def own(phase, part):
        for region in ORDER["x"]:
            for link in onward((phase, "0", region, part)):
                queue[link].append((phase, "0", region, part))

    for phase in range(len(toks)):
        own(phase, 0)
        post(1.6 + 0.5 * phase, ("own", phase))
    while True:
        while coming and coming[0][0] <= now:
            kind, key = heapq.heappop(coming)[2]
            if kind == "piece":
                have.add(("here", key))
                steps.append(("take", key))
                for link in onward(key):
                    queue[link].append(key)
                busy["pair"] = max(busy["pair"], now) + size(key) / pair_rate
                post(busy["pair"] + pair_hop, ("there", key))
                now += 2 * issue
            elif kind == "own":
                steps.append(("own", key))
                own(key, 1)
            else:
                have.add((kind, key))
            pump()
        pump()
        ready = [task for task in tasks if all(need in have for need in task[2])]
        if ready:
            name, took, _, reply = ready[0]
            tasks.remove(ready[0])
            steps.append(("task", name))
            now += took
            have.add(("done", name))
            if reply:
                post(now + reply, ("reply", name))
        elif coming:
            now = max(now, coming[0][0])
        else:
            break
    assert not tasks and not any(queue.values())
    return steps


def tiles_of(tok):
    return {64: (("0",), ("R",), ("2",), ("L",)), 32: (("0", "R"), ("2", "L")), 16: (BLOCKS,)}[tok]


def make_tasks(toks, cols, grad_steps):
    tasks = []
    n = len(toks)
    for phase, tok in enumerate(toks):
        scale = tok / 32
        tasks.append((("merge1", phase), 0.2, (("reply", ("stats", phase)),), 4.5))
        tasks.append((("merge2", phase), 0.2, (("reply", ("merge1", phase)),), 0))
        tasks.append((("slope", phase), 0.1 + 0.3 * scale, (("done", ("merge2", phase)),), 0))
    for phase, tok in enumerate(toks):
        scale = tok / 32
        names = []
        for region in REGIONS:
            for tile in tiles_of(tok):
                name = ("logits", phase, region, tile)
                keys = [
                    (phase, block, region, part)
                    for b in tile for block in (("Z0",) if b == "0" else (b, "Z" + b)) for part in (0, 1)
                ]
                needs = [("here", key) for key in keys] + [("there", key) for key in keys]
                took = 0.1 + tok / 32 * len(tile) / 4 * 3.9 * cols[phase][region] / (24 * LANES)
                tasks.append((name, took, tuple(needs), 0))
                names.append(("done", name))
        tasks.append((("stats", phase), 0.1 + 0.25 * scale, tuple(names), 5.0))
    for phase, tok in enumerate(toks[:-1]):
        for i in range(grad_steps):
            tasks.append((("grad", phase, i), 0.1 + 3.2 * tok / 32 / grad_steps, (("done", ("slope", phase)),), 0))
    return tasks


def rectangle(total, rows, cols):
    return next((a, total // a) for a in range(1, rows + 1) if total % a == 0 and total // a <= cols)


def remote(src, dst, send_sem, recv_sem, device):
    return pltpu.make_async_remote_copy(
        src_ref=src, dst_ref=dst, send_sem=send_sem, recv_sem=recv_sem, device_id=device, device_id_type=MESH)


def gather_head(hidden, labels, head_weight):
    depth, n_cols = head_weight.shape
    half = depth // 2
    unit = half // sum(SIZES[0])
    toks = TOKENS_OF
    n_phase = len(toks)
    offs = [sum(toks[:i]) for i in range(n_phase)]
    cols = [dict(zip(REGIONS, (unit * s for s in sizes))) for sizes in SIZES]
    starts = [{r: sum(c[o] for o in REGIONS[:i]) for i, r in enumerate(REGIONS)} for c in cols]
    grad_step = 1024
    foreign = BLOCKS[1:] + tuple("Z" + b for b in BLOCKS)
    keys = [(p, b, r, part) for p in range(n_phase) for b in foreign for r in REGIONS for part in (0, 1)]
    sem_of = {key: i for i, key in enumerate(keys)}
    groups = [(p, b, r) for p in range(n_phase) for b in BLOCKS for r in REGIONS]
    group_of = {g: i for i, g in enumerate(groups)}
    steps = plan(toks, cols, make_tasks(toks, cols, depth // grad_step))
    width = [max(4 * t, 256) if t == 16 else 4 * t for t in toks]
    n_block = [N_CTX * t // w for t, w in zip(toks, width)]
    n_row = [N_CTX * t // LANES for t in toks]

    def kernel(hid_hbm, lab_ref, w_hbm, grad, h_last, st_last, loss, *scratch):
        scratch = list(scratch)
        H = [scratch.pop(0) for _ in range(n_phase - 1)] + [h_last]
        ST = [scratch.pop(0) for _ in range(n_phase - 1)] + [st_last]
        LT = [scratch.pop(0) for _ in range(n_phase)]
        S1 = [scratch.pop(0) for _ in range(n_phase)]
        S2 = [scratch.pop(0) for _ in range(n_phase)]
        LP = [scratch.pop(0) for _ in range(n_phase)]
        LR = [scratch.pop(0) for _ in range(n_phase)]
        (W, LB, hid_sem, w_sem, recv, pair_recv, own_recv, rest_recv, send, own_send, st_send, st_recv, lb_send,
         lb_recv) = scratch
        ctx, voc = lax.axis_index("ctx"), lax.axis_index("vocab")
        core, zl, x = ctx % 2, (ctx // 2) % 2, ctx // 4
        zh, y = voc % 2, voc // 2
        q = y % 2

        def at(xx, zz, cc):
            return (xx * 2 + zz) * 2 + cc

        right, left, across = (x + 1) % 4, (x + 3) % 4, (x + 2) % 4
        zp, zm = (zh * 2 + zl + 1) % 4, (zh * 2 + zl + 3) % 4
        pair = (at(x, zl, 1 - core), voc)
        device = {
            "x+": (at(right, zl, core), voc),
            "x-": (at(left, zl, core), voc),
            "z+": (at(x, zp % 2, core), y * 2 + zp // 2),
            "z-": (at(x, zm % 2, core), y * 2 + zm // 2),
            "y+": (ctx, (voc + 2) % N_VOCAB),
            "y-": (ctx, (voc + 6) % N_VOCAB),
        }
        ctx_peers = [((ctx + i) % N_CTX, voc) for i in range(1, N_CTX)]
        voc_peers = [(ctx, (voc + i) % N_VOCAB) for i in range(1, N_VOCAB)]
        cross = (at(x, 1 - zl, core), y * 2 + 1 - zh)
        barrier = pltpu.get_barrier_semaphore()
        greeted = ctx_peers + voc_peers + [cross]
        for peer in greeted:
            pl.semaphore_signal(barrier, inc=1, device_id=peer, device_id_type=MESH)

        def own_rows(phase, which):
            return pl.ds(pl.multiple_of(at(x, zl, which) * toks[phase], 16), toks[phase])

        def load(phase):
            return pltpu.make_async_copy(
                hid_hbm.at[pl.ds(offs[phase], toks[phase]), :], H[phase].at[own_rows(phase, core), :],
                hid_sem.at[phase])

        for phase in range(n_phase):
            load(phase).start()
        w_load = pltpu.make_async_copy(w_hbm, W, w_sem)
        w_load.start()
        LB[ctx] = lab_ref[...]
        xs = {"0": x, "L": left, "R": right, "2": across}

        def region_at(phase, region, which):
            ahead = starts[phase][region]
            back = half - ahead - cols[phase][region]
            return pl.multiple_of(which * half + jnp.where(q == 0, ahead, back), LANES)

        def piece(key):
            phase, block, region, part = key
            xb = xs[block[-1]]
            zb = 1 - zl if block[0] == "Z" else zl
            row = at(xb, zb, 1 - core if part else core) * toks[phase]
            return H[phase].at[
                pl.ds(pl.multiple_of(row, 16), toks[phase]),
                pl.ds(region_at(phase, region, core), cols[phase][region])]

        def link_copy(link, key):
            ref = piece(key)
            return remote(ref, ref, send.at[key[0], LINKS.index(link)], recv.at[sem_of[landing(link, key)]],
                          device[link])

        def take(key):
            ref = piece(key)
            phase, block, region, _ = key
            remote(ref, ref, send.at[phase, 6], recv.at[sem_of[key]], pair).wait_recv()
            remote(ref, ref, send.at[phase, 6], pair_recv.at[group_of[(phase, block[-1], region)]], pair).start()

        def drain(phase, a, b, sem):
            ref = H[phase].at[pl.ds(0, a), pl.ds(0, b)]
            return remote(ref, ref, sem, sem, pair)

        def own_copy(phase, theirs):
            first = pl.multiple_of((1 - core if theirs else core) * half, LANES)
            ref = H[phase].at[own_rows(phase, core), pl.ds(first, half)]
            return remote(ref, ref, own_send.at[phase], (own_recv if theirs else rest_recv).at[phase], pair)

        def stat_copy(buf, phase, index, stage, peer):
            ref = buf[phase].at[index]
            return remote(ref, ref, st_send.at[phase, stage], st_recv.at[phase, stage], peer)

        def stat_all(buf, phase, stage, n):
            ref = buf[phase].at[pl.ds(0, n - 1)]
            return remote(ref, ref, st_send.at[phase, stage], st_recv.at[phase, stage], pair)

        def label_all():
            ref = LB.at[pl.ds(0, N_CTX - 1)]
            return remote(ref, ref, lb_send, lb_recv, pair)

        for phase in range(n_phase):
            load(phase).wait()
        pl.semaphore_wait(barrier, len(greeted))
        for phase in range(n_phase):
            own_copy(phase, True).start()
            own_copy(phase, False).start()

        first_col = (ctx * N_VOCAB + voc) * n_cols
        seen = set()

        def once(*what):
            new = what not in seen
            seen.add(what)
            return new

        def block_rows(phase, xb):
            n = 4 * toks[phase]
            return pl.ds(pl.multiple_of(xb * n, n), n)

        def logits_task(phase, region, tile):
            if once("w"):
                w_load.wait()
            for b in tile:
                if once("group", phase, b, region):
                    n = toks[phase] * (2 if b == "0" else 4)
                    drain(phase, n, cols[phase][region], pair_recv.at[group_of[(phase, b, region)]]).wait_recv()
                if b == "0" and once("rest", phase):
                    drain(phase, toks[phase], half, rest_recv.at[phase]).wait_recv()
            spans = [pl.ds(region_at(phase, region, which), cols[phase][region]) for which in (core, 1 - core)]
            whole = len(tile) == N_X
            rows = [block_rows(phase, xs[b]) for b in tile]
            left_side = jnp.concatenate([W[s, :] for s in spans], axis=0)
            if whole:
                right_side = jnp.concatenate([H[phase][:, s] for s in spans], axis=1)
            else:
                right_side = jnp.concatenate(
                    [jnp.concatenate([H[phase][r, s] for s in spans], axis=1) for r in rows], axis=0)
            part = lax.dot_general(
                left_side, right_side, (((0,), (1,)), ((), ())), preferred_element_type=jnp.float32)
            for i, b in enumerate(tile[:1] if whole else tile):
                piece_of = part if whole else part[:, i * width[phase]:(i + 1) * width[phase]]
                where = 0 if whole else xs[b]
                if region == REGIONS[0]:
                    LT[phase][where] = piece_of
                else:
                    LT[phase][where] += piece_of

        def label_mask(phase, i):
            ids = lax.broadcasted_iota(jnp.int32, (n_cols, width[phase]), 0)
            return ids == LR[phase][i] - first_col

        def label_rows():
            label_all().wait_recv()
            for phase, tok in enumerate(toks):
                per = width[phase] // tok
                for i in range(n_block[phase]):
                    LR[phase][i] = jnp.concatenate(
                        [LB[i * per + j][:, offs[phase]:offs[phase] + tok] for j in range(per)], axis=1)

        def stats_task(phase):
            if once("labels"):
                label_rows()
            per = width[phase] // LANES
            for i in range(n_block[phase]):
                lt = LT[phase][i]
                top = jnp.max(lt, axis=0, keepdims=True)
                total = jnp.sum(jnp.exp(lt - top), axis=0, keepdims=True)
                label = jnp.sum(jnp.where(label_mask(phase, i), lt, 0.0), axis=0, keepdims=True)
                for k, row in enumerate((top, total, label)):
                    for j in range(per):
                        r = i * per + j
                        S1[phase][ctx, k, r:r + 1, :] = row[:, j * LANES:(j + 1) * LANES]
            for peer in ctx_peers:
                stat_copy(S1, phase, ctx, 0, peer).start()

        def merged(buf, n):
            tops = [buf[i, 0] for i in range(n)]
            top = tops[0]
            for t in tops[1:]:
                top = jnp.maximum(top, t)
            total = sum(buf[i, 1] * jnp.exp(tops[i] - top) for i in range(n))
            return top, total, sum(buf[i, 2] for i in range(n))

        def merge1_task(phase):
            stat_all(S1, phase, 0, N_CTX).wait_recv()
            for k, row in enumerate(merged(S1[phase], N_CTX)):
                S2[phase][voc, k] = row
            for peer in voc_peers:
                stat_copy(S2, phase, voc, 1, peer).start()

        def merge2_task(phase):
            stat_all(S2, phase, 1, N_VOCAB).wait_recv()
            top, total, label = merged(S2[phase], N_VOCAB)
            lp = top + jnp.log(total)
            LP[phase][0] = lp
            LP[phase][1] = lp - label + z_weight * lp * lp
            first = ctx * toks[phase]
            row = LP[phase][1, pl.ds(first // LANES, 1), :]
            row = pltpu.roll(row, (offs[phase] - first % LANES + LANES) % LANES, 1)
            lane = lax.broadcasted_iota(jnp.int32, (1, LANES), 1)
            mine = (lane >= offs[phase]) & (lane < offs[phase] + toks[phase])
            loss[...] = jnp.where(mine, row, loss[...])

        def slope_task(phase):
            per = width[phase] // LANES
            for i in range(n_block[phase]):
                lp = jnp.concatenate([LP[phase][0, i * per + j:i * per + j + 1, :] for j in range(per)], axis=1)
                soft = jnp.exp(LT[phase][i] - lp)
                hot = jnp.where(label_mask(phase, i), 1.0, 0.0)
                ST[phase][:, i * width[phase]:(i + 1) * width[phase]] = (
                    (1.0 + 2.0 * z_weight * lp) * soft - hot).astype(jnp.bfloat16)

        def grad_task(phase, i):
            rs = pl.ds(i * grad_step, grad_step)
            part = lax.dot_general(
                H[phase][:, rs], ST[phase][...], (((0,), (1,)), ((), ())), preferred_element_type=jnp.float32)
            if phase == 0:
                grad[rs, :] = part
            else:
                grad[rs, :] += part

        run = {"logits": logits_task, "stats": stats_task, "merge1": merge1_task, "merge2": merge2_task,
               "slope": slope_task, "grad": grad_task}
        loss[...] = jnp.zeros_like(loss)
        for step in steps:
            if step[0] == "send":
                link_copy(step[1], step[2]).start()
            elif step[0] == "take":
                take(step[1])
            elif step[0] == "own":
                drain(step[1], toks[step[1]], half, own_recv.at[step[1]]).wait_recv()
                if step[1] == 0:
                    for peer in ctx_peers:
                        remote(LB.at[ctx], LB.at[ctx], lb_send, lb_recv, peer).start()
            else:
                run[step[1][0]](*step[1][1:])

        for phase in range(n_phase):
            for i, link in enumerate(LINKS):
                total = sum(cols[phase][s[2][2]] // unit for s in steps
                            if s[0] == "send" and s[1] == link and s[2][0] == phase)
                a, b = rectangle(total, N_CTX, depth // unit)
                drain(phase, a * toks[phase], b * unit, send.at[phase, i]).wait_send()
            drain(phase, 14 * toks[phase], half, send.at[phase, 6]).wait_send()
            drain(phase, toks[phase], depth, own_send.at[phase]).wait_send()
            stat_all(S1, phase, 0, N_CTX).wait_send()
            stat_all(S2, phase, 1, N_VOCAB).wait_send()
        label_all().wait_send()

    bf16, f32, i32 = jnp.bfloat16, jnp.float32, jnp.int32
    dma = pltpu.SemaphoreType.DMA
    vmem = pl.BlockSpec(memory_space=pltpu.VMEM)
    tokens = [N_CTX * t for t in toks]
    return pl.pallas_call(
        kernel,
        name="gather_head",
        out_shape=(pltpu.VMEM((depth, n_cols), f32), pltpu.VMEM((tokens[-1], depth), bf16),
                   pltpu.VMEM((n_cols, tokens[-1]), bf16), pltpu.VMEM((1, LANES), f32)),
        in_specs=[pl.BlockSpec(memory_space=pl.ANY), vmem, pl.BlockSpec(memory_space=pl.ANY)],
        out_specs=(vmem,) * 4,
        scratch_shapes=[
            *(pltpu.VMEM((n, depth), bf16) for n in tokens[:-1]),
            *(pltpu.VMEM((n_cols, n), bf16) for n in tokens[:-1]),
            *(pltpu.VMEM((n, n_cols, w), f32) for n, w in zip(n_block, width)),
            *(pltpu.VMEM((N_CTX, 3, n, LANES), f32) for n in n_row),
            *(pltpu.VMEM((N_VOCAB, 3, n, LANES), f32) for n in n_row),
            *(pltpu.VMEM((2, n, LANES), f32) for n in n_row),
            *(pltpu.VMEM((n, 1, w), i32) for n, w in zip(n_block, width)),
            pltpu.VMEM((depth, n_cols), bf16),
            pltpu.VMEM((N_CTX, 1, LANES), i32),
            dma((n_phase,)), dma, dma((len(keys),)), dma((len(groups),)), dma((n_phase,)), dma((n_phase,)),
            dma((n_phase, 7)), dma((n_phase,)), dma((n_phase, 2)), dma((n_phase, 2)), dma, dma,
        ],
        compiler_params=pltpu.CompilerParams(
            collective_id=0, has_side_effects=True, vmem_limit_bytes=42 * 2**20),
    )(hidden, labels.reshape(1, LANES), head_weight)


def finish(grad, h_last, st_last, loss):
    depth, n_cols = grad.shape
    step, slots = 1024, 3
    n = depth // step

    def kernel(grad_ref, h_ref, st_ref, loss_ref, out, loss_out, buf, sem):
        def copy(i):
            return pltpu.make_async_copy(buf.at[i % slots], out.at[pl.ds(i * step, step), :], sem.at[i % slots])

        loss_out[...] = loss_ref[...]
        for i in range(n):
            if i >= slots:
                copy(i - slots).wait()
            rs = pl.ds(i * step, step)
            buf[i % slots] = grad_ref[rs, :] + lax.dot_general(
                h_ref[:, rs], st_ref[...], (((0,), (1,)), ((), ())), preferred_element_type=jnp.float32)
            copy(i).start()
        for i in range(max(0, n - slots), n):
            copy(i).wait()

    vmem = pl.BlockSpec(memory_space=pltpu.VMEM)
    return pl.pallas_call(
        kernel,
        name="finish",
        out_shape=(jax.ShapeDtypeStruct((depth, n_cols), jnp.float32), jax.ShapeDtypeStruct((1, LANES), jnp.float32)),
        in_specs=[vmem] * 4,
        out_specs=(pl.BlockSpec(memory_space=pl.ANY), vmem),
        scratch_shapes=[pltpu.VMEM((slots, step, n_cols), jnp.float32), pltpu.SemaphoreType.DMA((slots,))],
        compiler_params=pltpu.CompilerParams(vmem_limit_bytes=16 * 2**20),
    )(grad, h_last, st_last, loss)


def head(hidden, labels, head_weight):
    parts = gather_head(hidden, labels, head_weight)
    parts = [pltpu.with_memory_space_constraint(p, pltpu.VMEM) for p in parts]
    grad, loss = finish(*parts)
    return loss.reshape(labels.shape), grad


def solution(mesh):
    return jax.shard_map(
        head,
        mesh=mesh,
        in_specs=(P("ctx", None), P("ctx"), P(None, ("ctx", "vocab"))),
        out_specs=(P("ctx"), P(None, ("ctx", "vocab"))),
        check_vma=False,
    )
```

```python
import heapq
import jax
import jax.numpy as jnp
from jax import lax
from jax.experimental import pallas as pl
from jax.experimental.pallas import tpu as pltpu
from jax.sharding import PartitionSpec as P

MESH = pl.DeviceIdType.MESH
z_weight = 0.0001

TOKENS_OF = (32, 64, 32)
SIZES = ((4, 5, 6, 5, 4), (5, 5, 4, 5, 5), (5, 5, 4, 5, 5))
REGIONS = ("F", "F'", "C", "S'", "S")
BLOCKS = ("0", "R", "2", "L")
LINKS = ("x+", "x-", "z+", "z-", "y+", "y-")
ORDER = {"x": ("F", "F'", "C", "S'"), "z": ("F", "F'", "C"), "y": ("F", "F'")}
NEAR = {"0": 0, "L": 1, "R": 1, "2": 2}
LANES = 128
N_CTX, N_VOCAB, N_X = 16, 8, 4


def onward(key):
    _, block, region, part = key
    links = []
    if block[0] != "Z":
        if region != "S":
            if block == "0":
                links += ["x+", "x-"]
            if (block, part) == ("L", 0):
                links.append("x+")
            if (block, part) == ("R", 1):
                links.append("x-")
        if region in ORDER["z"]:
            links.append(("z+", "z-")[part])
        if region == "F" and block != "0":
            links.append(("y+", "y-")[part])
    elif region in ORDER["y"]:
        links.append(("y+", "y-")[part])
    return links


def landing(link, key):
    phase, block, region, part = key
    if link[0] == "x":
        block = "2" if block != "0" else ("L" if link == "x+" else "R")
    elif link[0] == "z":
        block = "Z" + block
    else:
        region = {"F": "S", "F'": "S'"}[region]
    return phase, block, region, part


def rank(link, key):
    return key[0], ORDER[link[0]].index(key[2]), NEAR[key[1][-1]], key[3]


def plan(toks, cols, tasks):
    link_rate, pair_rate, hop, pair_hop, issue, ahead = 43e3, 500e3, 3.0, 1.5, 0.03, 5.0
    now, tick = 0.0, 0
    busy = dict.fromkeys(LINKS + ("pair",), 0.0)
    busy["pair"] = 3.2
    queue = {link: [] for link in LINKS}
    coming, have, steps = [], set(), []
    tasks = list(tasks)

    def post(when, what):
        nonlocal tick
        tick += 1
        heapq.heappush(coming, (when, tick, what))

    def size(key):
        return 2 * toks[key[0]] * cols[key[0]][key[2]]

    def pump():
        nonlocal now
        for link in LINKS:
            while queue[link] and busy[link] - now < ahead:
                key = min(queue[link], key=lambda k: rank(link, k))
                queue[link].remove(key)
                steps.append(("send", link, key))
                now += issue
                busy[link] = max(busy[link], now) + size(key) / link_rate
                post(busy[link] + hop, ("piece", landing(link, key)))

    def own(phase, part):
        for region in ORDER["x"]:
            for link in onward((phase, "0", region, part)):
                queue[link].append((phase, "0", region, part))

    for phase in range(len(toks)):
        own(phase, 0)
        post(1.6 + 0.5 * phase, ("own", phase))
    while True:
        while coming and coming[0][0] <= now:
            kind, key = heapq.heappop(coming)[2]
            if kind == "piece":
                have.add(("here", key))
                steps.append(("take", key))
                for link in onward(key):
                    queue[link].append(key)
                busy["pair"] = max(busy["pair"], now) + size(key) / pair_rate
                post(busy["pair"] + pair_hop, ("there", key))
                now += 2 * issue
            elif kind == "own":
                steps.append(("own", key))
                own(key, 1)
            else:
                have.add((kind, key))
            pump()
        pump()
        ready = [task for task in tasks if all(need in have for need in task[2])]
        if ready:
            name, took, _, reply = ready[0]
            tasks.remove(ready[0])
            steps.append(("task", name))
            now += took
            have.add(("done", name))
            if reply:
                post(now + reply, ("reply", name))
        elif coming:
            now = max(now, coming[0][0])
        else:
            break
    assert not tasks and not any(queue.values())
    return steps


def tiles_of(tok):
    return {64: (("0", "R"), ("2", "L")), 32: (("0", "R"), ("2", "L"))}[tok]


def make_tasks(toks, cols, grad_steps):
    tasks = []
    n = len(toks)
    for phase, tok in enumerate(toks):
        scale = tok / 32
        tasks.append((("merge1", phase), 0.2, (("reply", ("stats", phase)),), 4.5))
        tasks.append((("merge2", phase), 0.2, (("reply", ("merge1", phase)),), 0))
        tasks.append((("slope", phase), 0.1 + 0.3 * scale, (("done", ("merge2", phase)),), 0))
    for phase, tok in enumerate(toks):
        scale = tok / 32
        names = []
        for region in REGIONS:
            for tile in tiles_of(tok):
                name = ("logits", phase, region, tile)
                keys = [
                    (phase, block, region, part)
                    for b in tile for block in (("Z0",) if b == "0" else (b, "Z" + b)) for part in (0, 1)
                ]
                needs = [("here", key) for key in keys] + [("there", key) for key in keys]
                took = 0.1 + 3.9 * scale * len(tile) / 4 * cols[phase][region] / (24 * LANES)
                tasks.append((name, took, tuple(needs), 0))
                names.append(("done", name))
        tasks.append((("stats", phase), 0.1 + 0.25 * scale, tuple(names), 5.0))
    for phase, tok in enumerate(toks[:-1]):
        for i in range(grad_steps):
            tasks.append((("grad", phase, i), 0.1 + 3.2 * tok / 32 / grad_steps, (("done", ("slope", phase)),), 0))
    return tasks


def rectangle(total, rows, cols):
    return next((a, total // a) for a in range(1, rows + 1) if total % a == 0 and total // a <= cols)


def remote(src, dst, send_sem, recv_sem, device):
    return pltpu.make_async_remote_copy(
        src_ref=src, dst_ref=dst, send_sem=send_sem, recv_sem=recv_sem, device_id=device, device_id_type=MESH)


def gather_head(hidden, labels, head_weight):
    depth, n_cols = head_weight.shape
    half = depth // 2
    unit = half // sum(SIZES[0])
    toks = TOKENS_OF
    n_phase = len(toks)
    offs = [sum(toks[:i]) for i in range(n_phase)]
    cols = [dict(zip(REGIONS, (unit * s for s in sizes))) for sizes in SIZES]
    starts = [{r: sum(c[o] for o in REGIONS[:i]) for i, r in enumerate(REGIONS)} for c in cols]
    grad_step = 1024
    foreign = BLOCKS[1:] + tuple("Z" + b for b in BLOCKS)
    keys = [(p, b, r, part) for p in range(n_phase) for b in foreign for r in REGIONS for part in (0, 1)]
    sem_of = {key: i for i, key in enumerate(keys)}
    groups = [(p, b, r) for p in range(n_phase) for b in BLOCKS for r in REGIONS]
    group_of = {g: i for i, g in enumerate(groups)}
    steps = plan(toks, cols, make_tasks(toks, cols, depth // grad_step))
    joined = []
    for step in steps:
        if step[0] == "task" and step[1][0] == "grad":
            _, phase, i = step[1]
            if joined and joined[-1][0] == "task" and joined[-1][1][:2] == ("grad", phase):
                joined[-1] = ("task", ("grad", phase, joined[-1][1][2], i))
                continue
            step = ("task", ("grad", phase, i, i))
        joined.append(step)
    steps = joined
    width = [max(4 * t, 256) if t == 16 else 4 * t for t in toks]
    n_block = [N_CTX * t // w for t, w in zip(toks, width)]
    n_row = [N_CTX * t // LANES for t in toks]

    def kernel(hid_hbm, lab_ref, w_hbm, grad, h_last, st_last, loss, *scratch):
        scratch = list(scratch)
        H = [scratch.pop(0) for _ in range(n_phase - 1)] + [h_last]
        ST = [scratch.pop(0) for _ in range(n_phase - 1)] + [st_last]
        LT = [scratch.pop(0) for _ in range(n_phase)]
        S1 = [scratch.pop(0) for _ in range(n_phase)]
        S2 = [scratch.pop(0) for _ in range(n_phase)]
        LP = [scratch.pop(0) for _ in range(n_phase)]
        LR = [scratch.pop(0) for _ in range(n_phase)]
        (W, LB, hid_sem, w_sem, recv, pair_recv, own_recv, rest_recv, send, own_send, st_send, st_recv, lb_send,
         lb_recv) = scratch
        ctx, voc = lax.axis_index("ctx"), lax.axis_index("vocab")
        core, zl, x = ctx % 2, (ctx // 2) % 2, ctx // 4
        zh, y = voc % 2, voc // 2
        q = y % 2

        def at(xx, zz, cc):
            return (xx * 2 + zz) * 2 + cc

        right, left, across = (x + 1) % 4, (x + 3) % 4, (x + 2) % 4
        zp, zm = (zh * 2 + zl + 1) % 4, (zh * 2 + zl + 3) % 4
        pair = (at(x, zl, 1 - core), voc)
        device = {
            "x+": (at(right, zl, core), voc),
            "x-": (at(left, zl, core), voc),
            "z+": (at(x, zp % 2, core), y * 2 + zp // 2),
            "z-": (at(x, zm % 2, core), y * 2 + zm // 2),
            "y+": (ctx, (voc + 2) % N_VOCAB),
            "y-": (ctx, (voc + 6) % N_VOCAB),
        }
        ctx_peers = [((ctx + i) % N_CTX, voc) for i in range(1, N_CTX)]
        voc_peers = [(ctx, (voc + i) % N_VOCAB) for i in range(1, N_VOCAB)]
        cross = (at(x, 1 - zl, core), y * 2 + 1 - zh)
        barrier = pltpu.get_barrier_semaphore()
        greeted = ctx_peers + voc_peers + [cross]
        for peer in greeted:
            pl.semaphore_signal(barrier, inc=1, device_id=peer, device_id_type=MESH)

        def own_rows(phase, which):
            return pl.ds(pl.multiple_of(at(x, zl, which) * toks[phase], 16), toks[phase])

        def load(phase):
            return pltpu.make_async_copy(
                hid_hbm.at[pl.ds(offs[phase], toks[phase]), :], H[phase].at[own_rows(phase, core), :],
                hid_sem.at[phase])

        for phase in range(n_phase):
            load(phase).start()
        w_load = pltpu.make_async_copy(w_hbm, W, w_sem)
        w_load.start()
        LB[ctx] = lab_ref[...]
        xs = {"0": x, "L": left, "R": right, "2": across}

        def region_at(phase, region, which):
            ahead = starts[phase][region]
            back = half - ahead - cols[phase][region]
            return pl.multiple_of(which * half + jnp.where(q == 0, ahead, back), LANES)

        def piece(key):
            phase, block, region, part = key
            xb = xs[block[-1]]
            zb = 1 - zl if block[0] == "Z" else zl
            row = at(xb, zb, 1 - core if part else core) * toks[phase]
            return H[phase].at[
                pl.ds(pl.multiple_of(row, 16), toks[phase]),
                pl.ds(region_at(phase, region, core), cols[phase][region])]

        def link_copy(link, key):
            ref = piece(key)
            return remote(ref, ref, send.at[key[0], LINKS.index(link)], recv.at[sem_of[landing(link, key)]],
                          device[link])

        def take(key):
            ref = piece(key)
            phase, block, region, _ = key
            remote(ref, ref, send.at[phase, 6], recv.at[sem_of[key]], pair).wait_recv()
            remote(ref, ref, send.at[phase, 6], pair_recv.at[group_of[(phase, block[-1], region)]], pair).start()

        def drain(phase, a, b, sem):
            ref = H[phase].at[pl.ds(0, a), pl.ds(0, b)]
            return remote(ref, ref, sem, sem, pair)

        def own_copy(phase, theirs):
            first = pl.multiple_of((1 - core if theirs else core) * half, LANES)
            ref = H[phase].at[own_rows(phase, core), pl.ds(first, half)]
            return remote(ref, ref, own_send.at[phase], (own_recv if theirs else rest_recv).at[phase], pair)

        def stat_copy(buf, phase, index, stage, peer):
            ref = buf[phase].at[index]
            return remote(ref, ref, st_send.at[phase, stage], st_recv.at[phase, stage], peer)

        def stat_all(buf, phase, stage, n):
            ref = buf[phase].at[pl.ds(0, n - 1)]
            return remote(ref, ref, st_send.at[phase, stage], st_recv.at[phase, stage], pair)

        def label_all():
            ref = LB.at[pl.ds(0, N_CTX - 1)]
            return remote(ref, ref, lb_send, lb_recv, pair)

        for phase in range(n_phase):
            load(phase).wait()
        pl.semaphore_wait(barrier, len(greeted))
        for phase in range(n_phase):
            own_copy(phase, True).start()
            own_copy(phase, False).start()

        first_col = (ctx * N_VOCAB + voc) * n_cols
        seen = set()

        def once(*what):
            new = what not in seen
            seen.add(what)
            return new

        def block_rows(phase, xb):
            n = 4 * toks[phase]
            return pl.ds(pl.multiple_of(xb * n, n), n)

        def logits_task(phase, region, tile):
            if once("w"):
                w_load.wait()
            for b in tile:
                if once("group", phase, b, region):
                    n = toks[phase] * (2 if b == "0" else 4)
                    drain(phase, n, cols[phase][region], pair_recv.at[group_of[(phase, b, region)]]).wait_recv()
                if b == "0" and once("rest", phase):
                    drain(phase, toks[phase], half, rest_recv.at[phase]).wait_recv()
            spans = [pl.ds(region_at(phase, region, which), cols[phase][region]) for which in (core, 1 - core)]
            left_side = jnp.concatenate([W[k, :] for k in spans], axis=0)

            def product(blocks):
                rows = [block_rows(phase, xb) for xb in blocks]
                right_side = jnp.concatenate(
                    [jnp.concatenate([H[phase][r, k] for k in spans], axis=1) for r in rows], axis=0)
                part = lax.dot_general(
                    left_side, right_side, (((0,), (1,)), ((), ())), preferred_element_type=jnp.float32)
                for i, xb in enumerate(blocks):
                    piece_of = part[:, i * width[phase]:(i + 1) * width[phase]]
                    if region == REGIONS[0]:
                        LT[phase][xb] = piece_of
                    else:
                        LT[phase][xb] += piece_of

            if toks[phase] == 64:
                first = BLOCKS.index(tile[0])
                pl.loop(first, first + 2)(lambda i: product([lax.rem(x + i, N_X)]))
            else:
                product([xs[b] for b in tile])

        def label_mask(phase, i):
            ids = lax.broadcasted_iota(jnp.int32, (n_cols, width[phase]), 0)
            return ids == LR[phase][i] - first_col

        def label_rows():
            label_all().wait_recv()
            for phase, tok in enumerate(toks):
                per = width[phase] // tok
                for i in range(n_block[phase]):
                    LR[phase][i] = jnp.concatenate(
                        [LB[i * per + j][:, offs[phase]:offs[phase] + tok] for j in range(per)], axis=1)

        def stats_task(phase):
            if once("labels"):
                label_rows()
            per = width[phase] // LANES
            for i in range(n_block[phase]):
                lt = LT[phase][i]
                top = jnp.max(lt, axis=0, keepdims=True)
                total = jnp.sum(jnp.exp(lt - top), axis=0, keepdims=True)
                label = jnp.sum(jnp.where(label_mask(phase, i), lt, 0.0), axis=0, keepdims=True)
                for k, row in enumerate((top, total, label)):
                    for j in range(per):
                        r = i * per + j
                        S1[phase][ctx, k, r:r + 1, :] = row[:, j * LANES:(j + 1) * LANES]
            for peer in ctx_peers:
                stat_copy(S1, phase, ctx, 0, peer).start()

        def merged(buf, n):
            tops = [buf[i, 0] for i in range(n)]
            top = tops[0]
            for t in tops[1:]:
                top = jnp.maximum(top, t)
            total = sum(buf[i, 1] * jnp.exp(tops[i] - top) for i in range(n))
            return top, total, sum(buf[i, 2] for i in range(n))

        def merge1_task(phase):
            stat_all(S1, phase, 0, N_CTX).wait_recv()
            for k, row in enumerate(merged(S1[phase], N_CTX)):
                S2[phase][voc, k] = row
            for peer in voc_peers:
                stat_copy(S2, phase, voc, 1, peer).start()

        def merge2_task(phase):
            stat_all(S2, phase, 1, N_VOCAB).wait_recv()
            top, total, label = merged(S2[phase], N_VOCAB)
            lp = top + jnp.log(total)
            LP[phase][0] = lp
            LP[phase][1] = lp - label + z_weight * lp * lp
            first = ctx * toks[phase]
            row = LP[phase][1, pl.ds(first // LANES, 1), :]
            row = pltpu.roll(row, (offs[phase] - first % LANES + LANES) % LANES, 1)
            lane = lax.broadcasted_iota(jnp.int32, (1, LANES), 1)
            mine = (lane >= offs[phase]) & (lane < offs[phase] + toks[phase])
            loss[...] = jnp.where(mine, row, loss[...])

        def slope_task(phase):
            per = width[phase] // LANES
            for i in range(n_block[phase]):
                lp = jnp.concatenate([LP[phase][0, i * per + j:i * per + j + 1, :] for j in range(per)], axis=1)
                soft = jnp.exp(LT[phase][i] - lp)
                hot = jnp.where(label_mask(phase, i), 1.0, 0.0)
                ST[phase][:, i * width[phase]:(i + 1) * width[phase]] = (
                    (1.0 + 2.0 * z_weight * lp) * soft - hot).astype(jnp.bfloat16)

        def grad_run(phase, first, last):
            if first == last:
                grad_task(phase, first)
            else:
                pl.loop(first, last + 1)(lambda i: grad_task(phase, i))

        def grad_task(phase, i):
            rs = pl.ds(i * grad_step if isinstance(i, int) else pl.multiple_of(i * grad_step, grad_step), grad_step)
            part = lax.dot_general(
                H[phase][:, rs], ST[phase][...], (((0,), (1,)), ((), ())), preferred_element_type=jnp.float32)
            if phase == 0:
                grad[rs, :] = part
            else:
                grad[rs, :] += part

        run = {"logits": logits_task, "stats": stats_task, "merge1": merge1_task, "merge2": merge2_task,
               "slope": slope_task, "grad": grad_run}
        loss[...] = jnp.zeros_like(loss)
        for step in steps:
            if step[0] == "send":
                link_copy(step[1], step[2]).start()
            elif step[0] == "take":
                take(step[1])
            elif step[0] == "own":
                drain(step[1], toks[step[1]], half, own_recv.at[step[1]]).wait_recv()
                if step[1] == 0:
                    for peer in ctx_peers:
                        remote(LB.at[ctx], LB.at[ctx], lb_send, lb_recv, peer).start()
            else:
                run[step[1][0]](*step[1][1:])

        for phase in range(n_phase):
            for i, link in enumerate(LINKS):
                total = sum(cols[phase][s[2][2]] // unit for s in steps
                            if s[0] == "send" and s[1] == link and s[2][0] == phase)
                a, b = rectangle(total, N_CTX, depth // unit)
                drain(phase, a * toks[phase], b * unit, send.at[phase, i]).wait_send()
            drain(phase, 14 * toks[phase], half, send.at[phase, 6]).wait_send()
            drain(phase, toks[phase], depth, own_send.at[phase]).wait_send()
            stat_all(S1, phase, 0, N_CTX).wait_send()
            stat_all(S2, phase, 1, N_VOCAB).wait_send()
        label_all().wait_send()

    bf16, f32, i32 = jnp.bfloat16, jnp.float32, jnp.int32
    dma = pltpu.SemaphoreType.DMA
    vmem = pl.BlockSpec(memory_space=pltpu.VMEM)
    tokens = [N_CTX * t for t in toks]
    return pl.pallas_call(
        kernel,
        name="gather_head",
        out_shape=(pltpu.VMEM((depth, n_cols), f32), pltpu.VMEM((tokens[-1], depth), bf16),
                   pltpu.VMEM((n_cols, tokens[-1]), bf16), pltpu.VMEM((1, LANES), f32)),
        in_specs=[pl.BlockSpec(memory_space=pl.ANY), vmem, pl.BlockSpec(memory_space=pl.ANY)],
        out_specs=(vmem,) * 4,
        scratch_shapes=[
            *(pltpu.VMEM((n, depth), bf16) for n in tokens[:-1]),
            *(pltpu.VMEM((n_cols, n), bf16) for n in tokens[:-1]),
            *(pltpu.VMEM((n, n_cols, w), f32) for n, w in zip(n_block, width)),
            *(pltpu.VMEM((N_CTX, 3, n, LANES), f32) for n in n_row),
            *(pltpu.VMEM((N_VOCAB, 3, n, LANES), f32) for n in n_row),
            *(pltpu.VMEM((2, n, LANES), f32) for n in n_row),
            *(pltpu.VMEM((n, 1, w), i32) for n, w in zip(n_block, width)),
            pltpu.VMEM((depth, n_cols), bf16),
            pltpu.VMEM((N_CTX, 1, LANES), i32),
            dma((n_phase,)), dma, dma((len(keys),)), dma((len(groups),)), dma((n_phase,)), dma((n_phase,)),
            dma((n_phase, 7)), dma((n_phase,)), dma((n_phase, 2)), dma((n_phase, 2)), dma, dma,
        ],
        compiler_params=pltpu.CompilerParams(
            collective_id=0, has_side_effects=True, vmem_limit_bytes=42 * 2**20),
    )(hidden, labels.reshape(1, LANES), head_weight)


def finish(grad, h_last, st_last, loss):
    depth, n_cols = grad.shape
    step, slots = 1024, 3
    n = depth // step

    def kernel(grad_ref, h_ref, st_ref, loss_ref, out, loss_out, buf, sem):
        def copy(i):
            k = lax.rem(i, slots)
            return pltpu.make_async_copy(
                buf.at[k], out.at[pl.ds(pl.multiple_of(i * step, step), step), :], sem.at[k])

        loss_out[...] = loss_ref[...]

        @pl.loop(0, n)
        def _(i):
            @pl.when(i >= slots)
            def _():
                copy(i).wait()

            rs = pl.ds(pl.multiple_of(i * step, step), step)
            buf[lax.rem(i, slots)] = grad_ref[rs, :] + lax.dot_general(
                h_ref[:, rs], st_ref[...], (((0,), (1,)), ((), ())), preferred_element_type=jnp.float32)
            copy(i).start()

        for i in range(max(0, n - slots), n):
            copy(i).wait()

    vmem = pl.BlockSpec(memory_space=pltpu.VMEM)
    return pl.pallas_call(
        kernel,
        name="finish",
        out_shape=(jax.ShapeDtypeStruct((depth, n_cols), jnp.float32), jax.ShapeDtypeStruct((1, LANES), jnp.float32)),
        in_specs=[vmem] * 4,
        out_specs=(pl.BlockSpec(memory_space=pl.ANY), vmem),
        scratch_shapes=[pltpu.VMEM((slots, step, n_cols), jnp.float32), pltpu.SemaphoreType.DMA((slots,))],
        compiler_params=pltpu.CompilerParams(vmem_limit_bytes=16 * 2**20),
    )(grad, h_last, st_last, loss)


def head(hidden, labels, head_weight):
    parts = gather_head(hidden, labels, head_weight)
    parts = [pltpu.with_memory_space_constraint(p, pltpu.VMEM) for p in parts]
    grad, loss = finish(*parts)
    return loss.reshape(labels.shape), grad


def solution(mesh):
    return jax.shard_map(
        head,
        mesh=mesh,
        in_specs=(P("ctx", None), P("ctx"), P(None, ("ctx", "vocab"))),
        out_specs=(P("ctx"), P(None, ("ctx", "vocab"))),
        check_vma=False,
    )
```

```python
import heapq
import jax
import jax.numpy as jnp
from jax import lax
from jax.experimental import pallas as pl
from jax.experimental.pallas import tpu as pltpu
from jax.sharding import PartitionSpec as P

MESH = pl.DeviceIdType.MESH
z_weight = 0.0001

TOKENS_OF = (32, 64, 32)
SIZES = ((4, 5, 6, 5, 4), (5, 5, 4, 5, 5), (5, 5, 4, 5, 5))
REGIONS = ("F", "F'", "C", "S'", "S")
BLOCKS = ("0", "R", "2", "L")
LINKS = ("x+", "x-", "z+", "z-", "y+", "y-")
ORDER = {"x": ("F", "F'", "C", "S'"), "z": ("F", "F'", "C"), "y": ("F", "F'")}
NEAR = {"0": 0, "L": 1, "R": 1, "2": 2}
LANES = 128
N_CTX, N_VOCAB, N_X = 16, 8, 4


def onward(key):
    _, block, region, part = key
    links = []
    if block[0] != "Z":
        if region != "S":
            if block == "0":
                links += ["x+", "x-"]
            if (block, part) == ("L", 0):
                links.append("x+")
            if (block, part) == ("R", 1):
                links.append("x-")
        if region in ORDER["z"]:
            links.append(("z+", "z-")[part])
        if region == "F" and block != "0":
            links.append(("y+", "y-")[part])
    elif region in ORDER["y"]:
        links.append(("y+", "y-")[part])
    return links


def landing(link, key):
    phase, block, region, part = key
    if link[0] == "x":
        block = "2" if block != "0" else ("L" if link == "x+" else "R")
    elif link[0] == "z":
        block = "Z" + block
    else:
        region = {"F": "S", "F'": "S'"}[region]
    return phase, block, region, part


def rank(link, key):
    return key[0], ORDER[link[0]].index(key[2]), NEAR[key[1][-1]], key[3]


def plan(toks, cols, tasks):
    link_rate, pair_rate, hop, pair_hop, issue, ahead = 44e3, 500e3, 2.6, 1.5, 0.03, 3.5
    now, tick = 0.0, 0
    busy = dict.fromkeys(LINKS + ("pair",), 0.0)
    busy["pair"] = 3.2
    queue = {link: [] for link in LINKS}
    coming, have, steps = [], set(), []
    tasks = list(tasks)

    def post(when, what):
        nonlocal tick
        tick += 1
        heapq.heappush(coming, (when, tick, what))

    def size(key):
        return 2 * toks[key[0]] * cols[key[0]][key[2]]

    def pump():
        nonlocal now
        for link in LINKS:
            while queue[link] and busy[link] - now < ahead:
                key = min(queue[link], key=lambda k: rank(link, k))
                queue[link].remove(key)
                steps.append(("send", link, key))
                now += issue
                busy[link] = max(busy[link], now) + size(key) / link_rate
                post(busy[link] + hop, ("piece", landing(link, key)))

    def own(phase, part):
        for region in ORDER["x"]:
            for link in onward((phase, "0", region, part)):
                queue[link].append((phase, "0", region, part))

    for phase in range(len(toks)):
        own(phase, 0)
        post(1.6 + 0.5 * phase, ("own", phase))
    while True:
        while coming and coming[0][0] <= now:
            kind, key = heapq.heappop(coming)[2]
            if kind == "piece":
                have.add(("here", key))
                steps.append(("take", key))
                for link in onward(key):
                    queue[link].append(key)
                busy["pair"] = max(busy["pair"], now) + size(key) / pair_rate
                post(busy["pair"] + pair_hop, ("there", key))
                now += 2 * issue
            elif kind == "own":
                steps.append(("own", key))
                own(key, 1)
            else:
                have.add((kind, key))
            pump()
        pump()
        ready = [task for task in tasks if all(need in have for need in task[2])]
        if ready:
            name, took, _, reply = ready[0]
            tasks.remove(ready[0])
            steps.append(("task", name))
            now += took
            have.add(("done", name))
            if reply:
                post(now + reply, ("reply", name))
        elif coming:
            now = max(now, coming[0][0])
        else:
            break
    assert not tasks and not any(queue.values())
    return steps


def tiles_of(tok):
    return {64: (("0", "R"), ("2", "L")), 32: (("0", "R"), ("2", "L"))}[tok]


def make_tasks(toks, cols, grad_steps):
    tasks = []
    n = len(toks)
    for phase, tok in enumerate(toks):
        scale = tok / 32
        tasks.append((("merge1", phase), 0.2, (("reply", ("stats", phase)),), 4.5))
        tasks.append((("merge2", phase), 0.2, (("reply", ("merge1", phase)),), 0))
        tasks.append((("slope", phase), 0.1 + 0.3 * scale, (("done", ("merge2", phase)),), 0))
    for phase, tok in enumerate(toks):
        scale = tok / 32
        names = []
        for region in REGIONS:
            for tile in tiles_of(tok):
                name = ("logits", phase, region, tile)
                keys = [
                    (phase, block, region, part)
                    for b in tile for block in (("Z0",) if b == "0" else (b, "Z" + b)) for part in (0, 1)
                ]
                needs = [("here", key) for key in keys] + [("there", key) for key in keys]
                took = 0.1 + 3.9 * scale * len(tile) / 4 * cols[phase][region] / (24 * LANES)
                tasks.append((name, took, tuple(needs), 0))
                names.append(("done", name))
        tasks.append((("stats", phase), 0.1 + 0.25 * scale, tuple(names), 5.0))
    for phase, tok in enumerate(toks[:-1]):
        for i in range(grad_steps):
            tasks.append((("grad", phase, i), 0.1 + 3.2 * tok / 32 / grad_steps, (("done", ("slope", phase)),), 0))
    return tasks


def rectangle(total, rows, cols):
    return next((a, total // a) for a in range(1, rows + 1) if total % a == 0 and total // a <= cols)


def remote(src, dst, send_sem, recv_sem, device):
    return pltpu.make_async_remote_copy(
        src_ref=src, dst_ref=dst, send_sem=send_sem, recv_sem=recv_sem, device_id=device, device_id_type=MESH)


def gather_head(hidden, labels, head_weight):
    depth, n_cols = head_weight.shape
    half = depth // 2
    unit = half // sum(SIZES[0])
    toks = TOKENS_OF
    n_phase = len(toks)
    offs = [sum(toks[:i]) for i in range(n_phase)]
    cols = [dict(zip(REGIONS, (unit * s for s in sizes))) for sizes in SIZES]
    starts = [{r: sum(c[o] for o in REGIONS[:i]) for i, r in enumerate(REGIONS)} for c in cols]
    grad_step = 1024
    foreign = BLOCKS[1:] + tuple("Z" + b for b in BLOCKS)
    keys = [(p, b, r, part) for p in range(n_phase) for b in foreign for r in REGIONS for part in (0, 1)]
    sem_of = {key: i for i, key in enumerate(keys)}
    groups = [(p, b, r) for p in range(n_phase) for b in BLOCKS for r in REGIONS]
    group_of = {g: i for i, g in enumerate(groups)}
    steps = plan(toks, cols, make_tasks(toks, cols, depth // grad_step))
    joined = []
    for step in steps:
        if step[0] == "task" and step[1][0] == "grad":
            _, phase, i = step[1]
            if joined and joined[-1][0] == "task" and joined[-1][1][:2] == ("grad", phase):
                joined[-1] = ("task", ("grad", phase, joined[-1][1][2], i))
                continue
            step = ("task", ("grad", phase, i, i))
        joined.append(step)
    steps = joined
    width = [max(4 * t, 256) if t == 16 else 4 * t for t in toks]
    n_block = [N_CTX * t // w for t, w in zip(toks, width)]
    n_row = [N_CTX * t // LANES for t in toks]

    def kernel(hid_hbm, lab_ref, w_hbm, grad, h_last, st_last, loss, *scratch):
        scratch = list(scratch)
        H = [scratch.pop(0) for _ in range(n_phase - 1)] + [h_last]
        ST = [scratch.pop(0) for _ in range(n_phase - 1)] + [st_last]
        LT = [scratch.pop(0) for _ in range(n_phase)]
        S1 = [scratch.pop(0) for _ in range(n_phase)]
        S2 = [scratch.pop(0) for _ in range(n_phase)]
        LP = [scratch.pop(0) for _ in range(n_phase)]
        LR = [scratch.pop(0) for _ in range(n_phase)]
        (W, LB, hid_sem, w_sem, recv, pair_recv, own_recv, rest_recv, send, own_send, st_send, st_recv, lb_send,
         lb_recv) = scratch
        ctx, voc = lax.axis_index("ctx"), lax.axis_index("vocab")
        core, zl, x = ctx % 2, (ctx // 2) % 2, ctx // 4
        zh, y = voc % 2, voc // 2
        q = y % 2

        def at(xx, zz, cc):
            return (xx * 2 + zz) * 2 + cc

        right, left, across = (x + 1) % 4, (x + 3) % 4, (x + 2) % 4
        zp, zm = (zh * 2 + zl + 1) % 4, (zh * 2 + zl + 3) % 4
        pair = (at(x, zl, 1 - core), voc)
        device = {
            "x+": (at(right, zl, core), voc),
            "x-": (at(left, zl, core), voc),
            "z+": (at(x, zp % 2, core), y * 2 + zp // 2),
            "z-": (at(x, zm % 2, core), y * 2 + zm // 2),
            "y+": (ctx, (voc + 2) % N_VOCAB),
            "y-": (ctx, (voc + 6) % N_VOCAB),
        }
        ctx_peers = [((ctx + i) % N_CTX, voc) for i in range(1, N_CTX)]
        voc_peers = [(ctx, (voc + i) % N_VOCAB) for i in range(1, N_VOCAB)]
        cross = (at(x, 1 - zl, core), y * 2 + 1 - zh)
        barrier = pltpu.get_barrier_semaphore()
        greeted = ctx_peers + voc_peers + [cross]
        for peer in greeted:
            pl.semaphore_signal(barrier, inc=1, device_id=peer, device_id_type=MESH)

        def own_rows(phase, which):
            return pl.ds(pl.multiple_of(at(x, zl, which) * toks[phase], 16), toks[phase])

        def load(phase):
            return pltpu.make_async_copy(
                hid_hbm.at[pl.ds(offs[phase], toks[phase]), :], H[phase].at[own_rows(phase, core), :],
                hid_sem.at[phase])

        for phase in range(n_phase):
            load(phase).start()
        w_load = pltpu.make_async_copy(w_hbm, W, w_sem)
        w_load.start()
        LB[ctx] = lab_ref[...]
        xs = {"0": x, "L": left, "R": right, "2": across}

        def region_at(phase, region, which):
            ahead = starts[phase][region]
            back = half - ahead - cols[phase][region]
            return pl.multiple_of(which * half + jnp.where(q == 0, ahead, back), LANES)

        def piece(key):
            phase, block, region, part = key
            xb = xs[block[-1]]
            zb = 1 - zl if block[0] == "Z" else zl
            row = at(xb, zb, 1 - core if part else core) * toks[phase]
            return H[phase].at[
                pl.ds(pl.multiple_of(row, 16), toks[phase]),
                pl.ds(region_at(phase, region, core), cols[phase][region])]

        def link_copy(link, key):
            ref = piece(key)
            return remote(ref, ref, send.at[key[0], LINKS.index(link)], recv.at[sem_of[landing(link, key)]],
                          device[link])

        def take(key):
            ref = piece(key)
            phase, block, region, _ = key
            remote(ref, ref, send.at[phase, 6], recv.at[sem_of[key]], pair).wait_recv()
            remote(ref, ref, send.at[phase, 6], pair_recv.at[group_of[(phase, block[-1], region)]], pair).start()

        def drain(phase, a, b, sem):
            ref = H[phase].at[pl.ds(0, a), pl.ds(0, b)]
            return remote(ref, ref, sem, sem, pair)

        def own_copy(phase, theirs):
            first = pl.multiple_of((1 - core if theirs else core) * half, LANES)
            ref = H[phase].at[own_rows(phase, core), pl.ds(first, half)]
            return remote(ref, ref, own_send.at[phase], (own_recv if theirs else rest_recv).at[phase], pair)

        def stat_copy(buf, phase, index, stage, peer):
            ref = buf[phase].at[index]
            return remote(ref, ref, st_send.at[phase, stage], st_recv.at[phase, stage], peer)

        def stat_all(buf, phase, stage, n):
            ref = buf[phase].at[pl.ds(0, n - 1)]
            return remote(ref, ref, st_send.at[phase, stage], st_recv.at[phase, stage], pair)

        def label_all():
            ref = LB.at[pl.ds(0, N_CTX - 1)]
            return remote(ref, ref, lb_send, lb_recv, pair)

        for phase in range(n_phase):
            load(phase).wait()
        pl.semaphore_wait(barrier, len(greeted))
        for phase in range(n_phase):
            own_copy(phase, True).start()
            own_copy(phase, False).start()

        first_col = (ctx * N_VOCAB + voc) * n_cols
        seen = set()

        def once(*what):
            new = what not in seen
            seen.add(what)
            return new

        def block_rows(phase, xb):
            n = 4 * toks[phase]
            return pl.ds(pl.multiple_of(xb * n, n), n)

        def logits_task(phase, region, tile):
            if once("w"):
                w_load.wait()
            for b in tile:
                if once("group", phase, b, region):
                    n = toks[phase] * (2 if b == "0" else 4)
                    drain(phase, n, cols[phase][region], pair_recv.at[group_of[(phase, b, region)]]).wait_recv()
                if b == "0" and once("rest", phase):
                    drain(phase, toks[phase], half, rest_recv.at[phase]).wait_recv()
            spans = [pl.ds(region_at(phase, region, which), cols[phase][region]) for which in (core, 1 - core)]
            left_side = jnp.concatenate([W[k, :] for k in spans], axis=0)

            def product(blocks):
                rows = [block_rows(phase, xb) for xb in blocks]
                right_side = jnp.concatenate(
                    [jnp.concatenate([H[phase][r, k] for k in spans], axis=1) for r in rows], axis=0)
                part = lax.dot_general(
                    left_side, right_side, (((0,), (1,)), ((), ())), preferred_element_type=jnp.float32)
                for i, xb in enumerate(blocks):
                    piece_of = part[:, i * width[phase]:(i + 1) * width[phase]]
                    if region == REGIONS[0]:
                        LT[phase][xb] = piece_of
                    else:
                        LT[phase][xb] += piece_of

            if toks[phase] == 64:
                first = BLOCKS.index(tile[0])
                pl.loop(first, first + 2)(lambda i: product([lax.rem(x + i, N_X)]))
            else:
                product([xs[b] for b in tile])

        def label_mask(phase, i):
            ids = lax.broadcasted_iota(jnp.int32, (n_cols, width[phase]), 0)
            return ids == LR[phase][i] - first_col

        def label_rows():
            label_all().wait_recv()
            for phase, tok in enumerate(toks):
                per = width[phase] // tok
                for i in range(n_block[phase]):
                    LR[phase][i] = jnp.concatenate(
                        [LB[i * per + j][:, offs[phase]:offs[phase] + tok] for j in range(per)], axis=1)

        def stats_task(phase):
            if once("labels"):
                label_rows()
            per = width[phase] // LANES
            for i in range(n_block[phase]):
                lt = LT[phase][i]
                top = jnp.max(lt, axis=0, keepdims=True)
                total = jnp.sum(jnp.exp(lt - top), axis=0, keepdims=True)
                label = jnp.sum(jnp.where(label_mask(phase, i), lt, 0.0), axis=0, keepdims=True)
                for k, row in enumerate((top, total, label)):
                    for j in range(per):
                        r = i * per + j
                        S1[phase][ctx, k, r:r + 1, :] = row[:, j * LANES:(j + 1) * LANES]
            for peer in ctx_peers:
                stat_copy(S1, phase, ctx, 0, peer).start()

        def merged(buf, n):
            tops = [buf[i, 0] for i in range(n)]
            top = tops[0]
            for t in tops[1:]:
                top = jnp.maximum(top, t)
            total = sum(buf[i, 1] * jnp.exp(tops[i] - top) for i in range(n))
            return top, total, sum(buf[i, 2] for i in range(n))

        def merge1_task(phase):
            stat_all(S1, phase, 0, N_CTX).wait_recv()
            for k, row in enumerate(merged(S1[phase], N_CTX)):
                S2[phase][voc, k] = row
            for peer in voc_peers:
                stat_copy(S2, phase, voc, 1, peer).start()

        def merge2_task(phase):
            stat_all(S2, phase, 1, N_VOCAB).wait_recv()
            top, total, label = merged(S2[phase], N_VOCAB)
            lp = top + jnp.log(total)
            LP[phase][0] = lp
            LP[phase][1] = lp - label + z_weight * lp * lp
            first = ctx * toks[phase]
            row = LP[phase][1, pl.ds(first // LANES, 1), :]
            row = pltpu.roll(row, (offs[phase] - first % LANES + LANES) % LANES, 1)
            lane = lax.broadcasted_iota(jnp.int32, (1, LANES), 1)
            mine = (lane >= offs[phase]) & (lane < offs[phase] + toks[phase])
            loss[...] = jnp.where(mine, row, loss[...])

        def slope_task(phase):
            per = width[phase] // LANES
            for i in range(n_block[phase]):
                lp = jnp.concatenate([LP[phase][0, i * per + j:i * per + j + 1, :] for j in range(per)], axis=1)
                soft = jnp.exp(LT[phase][i] - lp)
                hot = jnp.where(label_mask(phase, i), 1.0, 0.0)
                ST[phase][:, i * width[phase]:(i + 1) * width[phase]] = (
                    (1.0 + 2.0 * z_weight * lp) * soft - hot).astype(jnp.bfloat16)

        def grad_run(phase, first, last):
            if first == last:
                grad_task(phase, first)
            else:
                pl.loop(first, last + 1)(lambda i: grad_task(phase, i))

        def grad_task(phase, i):
            rs = pl.ds(i * grad_step if isinstance(i, int) else pl.multiple_of(i * grad_step, grad_step), grad_step)
            part = lax.dot_general(
                H[phase][:, rs], ST[phase][...], (((0,), (1,)), ((), ())), preferred_element_type=jnp.float32)
            if phase == 0:
                grad[rs, :] = part
            else:
                grad[rs, :] += part

        run = {"logits": logits_task, "stats": stats_task, "merge1": merge1_task, "merge2": merge2_task,
               "slope": slope_task, "grad": grad_run}
        loss[...] = jnp.zeros_like(loss)
        for step in steps:
            if step[0] == "send":
                link_copy(step[1], step[2]).start()
            elif step[0] == "take":
                take(step[1])
            elif step[0] == "own":
                drain(step[1], toks[step[1]], half, own_recv.at[step[1]]).wait_recv()
                if step[1] == 0:
                    for peer in ctx_peers:
                        remote(LB.at[ctx], LB.at[ctx], lb_send, lb_recv, peer).start()
            else:
                run[step[1][0]](*step[1][1:])

        for phase in range(n_phase):
            for i, link in enumerate(LINKS):
                total = sum(cols[phase][s[2][2]] // unit for s in steps
                            if s[0] == "send" and s[1] == link and s[2][0] == phase)
                a, b = rectangle(total, N_CTX, depth // unit)
                drain(phase, a * toks[phase], b * unit, send.at[phase, i]).wait_send()
            drain(phase, 14 * toks[phase], half, send.at[phase, 6]).wait_send()
            drain(phase, toks[phase], depth, own_send.at[phase]).wait_send()
            stat_all(S1, phase, 0, N_CTX).wait_send()
            stat_all(S2, phase, 1, N_VOCAB).wait_send()
        label_all().wait_send()

    bf16, f32, i32 = jnp.bfloat16, jnp.float32, jnp.int32
    dma = pltpu.SemaphoreType.DMA
    vmem = pl.BlockSpec(memory_space=pltpu.VMEM)
    tokens = [N_CTX * t for t in toks]
    return pl.pallas_call(
        kernel,
        name="gather_head",
        out_shape=(pltpu.VMEM((depth, n_cols), f32), pltpu.VMEM((tokens[-1], depth), bf16),
                   pltpu.VMEM((n_cols, tokens[-1]), bf16), pltpu.VMEM((1, LANES), f32)),
        in_specs=[pl.BlockSpec(memory_space=pl.ANY), vmem, pl.BlockSpec(memory_space=pl.ANY)],
        out_specs=(vmem,) * 4,
        scratch_shapes=[
            *(pltpu.VMEM((n, depth), bf16) for n in tokens[:-1]),
            *(pltpu.VMEM((n_cols, n), bf16) for n in tokens[:-1]),
            *(pltpu.VMEM((n, n_cols, w), f32) for n, w in zip(n_block, width)),
            *(pltpu.VMEM((N_CTX, 3, n, LANES), f32) for n in n_row),
            *(pltpu.VMEM((N_VOCAB, 3, n, LANES), f32) for n in n_row),
            *(pltpu.VMEM((2, n, LANES), f32) for n in n_row),
            *(pltpu.VMEM((n, 1, w), i32) for n, w in zip(n_block, width)),
            pltpu.VMEM((depth, n_cols), bf16),
            pltpu.VMEM((N_CTX, 1, LANES), i32),
            dma((n_phase,)), dma, dma((len(keys),)), dma((len(groups),)), dma((n_phase,)), dma((n_phase,)),
            dma((n_phase, 7)), dma((n_phase,)), dma((n_phase, 2)), dma((n_phase, 2)), dma, dma,
        ],
        compiler_params=pltpu.CompilerParams(
            collective_id=0, has_side_effects=True, vmem_limit_bytes=42 * 2**20),
    )(hidden, labels.reshape(1, LANES), head_weight)


def finish(grad, h_last, st_last, loss):
    depth, n_cols = grad.shape
    step, slots = 1024, 3
    n = depth // step

    def kernel(grad_ref, h_ref, st_ref, loss_ref, out, loss_out, buf, sem):
        def copy(i):
            k = lax.rem(i, slots)
            return pltpu.make_async_copy(
                buf.at[k], out.at[pl.ds(pl.multiple_of(i * step, step), step), :], sem.at[k])

        loss_out[...] = loss_ref[...]

        @pl.loop(0, n)
        def _(i):
            @pl.when(i >= slots)
            def _():
                copy(i).wait()

            rs = pl.ds(pl.multiple_of(i * step, step), step)
            buf[lax.rem(i, slots)] = grad_ref[rs, :] + lax.dot_general(
                h_ref[:, rs], st_ref[...], (((0,), (1,)), ((), ())), preferred_element_type=jnp.float32)
            copy(i).start()

        for i in range(max(0, n - slots), n):
            copy(i).wait()

    vmem = pl.BlockSpec(memory_space=pltpu.VMEM)
    return pl.pallas_call(
        kernel,
        name="finish",
        out_shape=(jax.ShapeDtypeStruct((depth, n_cols), jnp.float32), jax.ShapeDtypeStruct((1, LANES), jnp.float32)),
        in_specs=[vmem] * 4,
        out_specs=(pl.BlockSpec(memory_space=pl.ANY), vmem),
        scratch_shapes=[pltpu.VMEM((slots, step, n_cols), jnp.float32), pltpu.SemaphoreType.DMA((slots,))],
        compiler_params=pltpu.CompilerParams(vmem_limit_bytes=16 * 2**20),
    )(grad, h_last, st_last, loss)


def head(hidden, labels, head_weight):
    parts = gather_head(hidden, labels, head_weight)
    parts = [pltpu.with_memory_space_constraint(p, pltpu.VMEM) for p in parts]
    grad, loss = finish(*parts)
    return loss.reshape(labels.shape), grad


def solution(mesh):
    return jax.shard_map(
        head,
        mesh=mesh,
        in_specs=(P("ctx", None), P("ctx"), P(None, ("ctx", "vocab"))),
        out_specs=(P("ctx"), P(None, ("ctx", "vocab"))),
        check_vma=False,
    )
```

```python
import heapq
import jax
import jax.numpy as jnp
from jax import lax
from jax.experimental import pallas as pl
from jax.experimental.pallas import tpu as pltpu
from jax.sharding import PartitionSpec as P

MESH = pl.DeviceIdType.MESH
z_weight = 0.0001

TOKENS_OF = (32, 64, 32)
SIZES = ((4, 5, 6, 5, 4), (5, 5, 4, 5, 5), (5, 5, 4, 5, 5))
REGIONS = ("F", "F'", "C", "S'", "S")
BLOCKS = ("0", "R", "2", "L")
LINKS = ("x+", "x-", "z+", "z-", "y+", "y-")
ORDER = {"x": ("F", "F'", "C", "S'"), "z": ("F", "F'", "C"), "y": ("F", "F'")}
NEAR = {"0": 0, "L": 1, "R": 1, "2": 2}
LANES = 128
N_CTX, N_VOCAB, N_X = 16, 8, 4


def onward(key):
    _, block, region, part = key
    links = []
    if block[0] != "Z":
        if region != "S":
            if block == "0":
                links += ["x+", "x-"]
            if (block, part) == ("L", 0):
                links.append("x+")
            if (block, part) == ("R", 1):
                links.append("x-")
        if region in ORDER["z"]:
            links.append(("z+", "z-")[part])
        if region == "F" and block != "0":
            links.append(("y+", "y-")[part])
    elif region in ORDER["y"]:
        links.append(("y+", "y-")[part])
    return links


def landing(link, key):
    phase, block, region, part = key
    if link[0] == "x":
        block = "2" if block != "0" else ("L" if link == "x+" else "R")
    elif link[0] == "z":
        block = "Z" + block
    else:
        region = {"F": "S", "F'": "S'"}[region]
    return phase, block, region, part


def rank(link, key):
    return key[0], ORDER[link[0]].index(key[2]), NEAR[key[1][-1]], key[3]


def plan(toks, cols, tasks):
    link_rate, pair_rate, hop, pair_hop, issue, ahead = 44e3, 500e3, 2.6, 1.5, 0.03, 3.5
    now, tick = 0.0, 0
    busy = dict.fromkeys(LINKS + ("pair",), 0.0)
    busy["pair"] = 3.2
    queue = {link: [] for link in LINKS}
    coming, have, steps = [], set(), []
    tasks = list(tasks)

    def post(when, what):
        nonlocal tick
        tick += 1
        heapq.heappush(coming, (when, tick, what))

    def size(key):
        return 2 * toks[key[0]] * cols[key[0]][key[2]]

    def pump():
        nonlocal now
        for link in LINKS:
            while queue[link] and busy[link] - now < ahead:
                key = min(queue[link], key=lambda k: rank(link, k))
                queue[link].remove(key)
                steps.append(("send", link, key))
                now += issue
                busy[link] = max(busy[link], now) + size(key) / link_rate
                post(busy[link] + hop, ("piece", landing(link, key)))

    def own(phase, part):
        for region in ORDER["x"]:
            for link in onward((phase, "0", region, part)):
                queue[link].append((phase, "0", region, part))

    for phase in range(len(toks)):
        own(phase, 0)
        post(1.6 + 0.5 * phase, ("own", phase))
    while True:
        while coming and coming[0][0] <= now:
            kind, key = heapq.heappop(coming)[2]
            if kind == "piece":
                have.add(("here", key))
                steps.append(("take", key))
                for link in onward(key):
                    queue[link].append(key)
                busy["pair"] = max(busy["pair"], now) + size(key) / pair_rate
                post(busy["pair"] + pair_hop, ("there", key))
                now += 2 * issue
            elif kind == "own":
                steps.append(("own", key))
                own(key, 1)
            else:
                have.add((kind, key))
            pump()
        pump()
        ready = [task for task in tasks if all(need in have for need in task[2])]
        if ready:
            name, took, _, reply = ready[0]
            tasks.remove(ready[0])
            steps.append(("task", name))
            now += took
            have.add(("done", name))
            if reply:
                post(now + reply, ("reply", name))
        elif coming:
            now = max(now, coming[0][0])
        else:
            break
    assert not tasks and not any(queue.values())
    return steps


def tiles_of(tok):
    return {64: (("0", "R"), ("2", "L")), 32: (("0", "R"), ("2", "L"))}[tok]


def make_tasks(toks, cols, grad_steps):
    tasks = []
    n = len(toks)
    for phase, tok in enumerate(toks):
        scale = tok / 32
        tasks.append((("merge1", phase), 0.2, (("reply", ("stats", phase)),), 4.5))
        tasks.append((("merge2", phase), 0.2, (("reply", ("merge1", phase)),), 0))
        tasks.append((("slope", phase), 0.1 + 0.3 * scale, (("done", ("merge2", phase)),), 0))
    for phase, tok in enumerate(toks):
        scale = tok / 32
        names = []
        for region in REGIONS:
            for tile in tiles_of(tok):
                name = ("logits", phase, region, tile)
                keys = [
                    (phase, block, region, part)
                    for b in tile for block in (("Z0",) if b == "0" else (b, "Z" + b)) for part in (0, 1)
                ]
                needs = [("here", key) for key in keys] + [("there", key) for key in keys]
                took = 0.1 + 3.9 * scale * len(tile) / 4 * cols[phase][region] / (24 * LANES)
                tasks.append((name, took, tuple(needs), 0))
                names.append(("done", name))
        tasks.append((("stats", phase), 0.1 + 0.25 * scale, tuple(names), 5.0))
    for phase, tok in enumerate(toks[:-1]):
        for i in range(grad_steps):
            tasks.append((("grad", phase, i), 0.1 + 3.2 * tok / 32 / grad_steps, (("done", ("slope", phase)),), 0))
    return tasks


def rectangle(total, rows, cols):
    return next((a, total // a) for a in range(1, rows + 1) if total % a == 0 and total // a <= cols)


def remote(src, dst, send_sem, recv_sem, device):
    return pltpu.make_async_remote_copy(
        src_ref=src, dst_ref=dst, send_sem=send_sem, recv_sem=recv_sem, device_id=device, device_id_type=MESH)


def gather_head(hidden, labels, head_weight):
    depth, n_cols = head_weight.shape
    half = depth // 2
    unit = half // sum(SIZES[0])
    toks = TOKENS_OF
    n_phase = len(toks)
    offs = [sum(toks[:i]) for i in range(n_phase)]
    cols = [dict(zip(REGIONS, (unit * s for s in sizes))) for sizes in SIZES]
    starts = [{r: sum(c[o] for o in REGIONS[:i]) for i, r in enumerate(REGIONS)} for c in cols]
    grad_step = 1024
    foreign = BLOCKS[1:] + tuple("Z" + b for b in BLOCKS)
    keys = [(p, b, r, part) for p in range(n_phase) for b in foreign for r in REGIONS for part in (0, 1)]
    sem_of = {key: i for i, key in enumerate(keys)}
    groups = [(p, b, r) for p in range(n_phase) for b in BLOCKS for r in REGIONS]
    group_of = {g: i for i, g in enumerate(groups)}
    steps = plan(toks, cols, make_tasks(toks, cols, depth // grad_step))
    joined = []
    for step in steps:
        if step[0] == "task" and step[1][0] == "grad":
            _, phase, i = step[1]
            if joined and joined[-1][0] == "task" and joined[-1][1][:2] == ("grad", phase):
                joined[-1] = ("task", ("grad", phase, joined[-1][1][2], i))
                continue
            step = ("task", ("grad", phase, i, i))
        joined.append(step)
    steps = joined
    width = [max(4 * t, 256) if t == 16 else 4 * t for t in toks]
    n_block = [N_CTX * t // w for t, w in zip(toks, width)]
    n_row = [N_CTX * t // LANES for t in toks]

    def kernel(hid_hbm, lab_ref, w_hbm, grad, h_last, st_last, loss, *scratch):
        scratch = list(scratch)
        H = [scratch.pop(0) for _ in range(n_phase - 1)] + [h_last]
        ST = [scratch.pop(0) for _ in range(n_phase - 1)] + [st_last]
        LT = [scratch.pop(0) for _ in range(n_phase)]
        S1 = [scratch.pop(0) for _ in range(n_phase)]
        S2 = [scratch.pop(0) for _ in range(n_phase)]
        LP = [scratch.pop(0) for _ in range(n_phase)]
        LR = [scratch.pop(0) for _ in range(n_phase)]
        (W, LB, hid_sem, w_sem, recv, pair_recv, own_recv, rest_recv, send, own_send, st_send, st_recv, lb_send,
         lb_recv) = scratch
        ctx, voc = lax.axis_index("ctx"), lax.axis_index("vocab")
        core, zl, x = ctx % 2, (ctx // 2) % 2, ctx // 4
        zh, y = voc % 2, voc // 2
        q = y % 2

        def at(xx, zz, cc):
            return (xx * 2 + zz) * 2 + cc

        right, left, across = (x + 1) % 4, (x + 3) % 4, (x + 2) % 4
        zp, zm = (zh * 2 + zl + 1) % 4, (zh * 2 + zl + 3) % 4
        pair = (at(x, zl, 1 - core), voc)
        device = {
            "x+": (at(right, zl, core), voc),
            "x-": (at(left, zl, core), voc),
            "z+": (at(x, zp % 2, core), y * 2 + zp // 2),
            "z-": (at(x, zm % 2, core), y * 2 + zm // 2),
            "y+": (ctx, (voc + 2) % N_VOCAB),
            "y-": (ctx, (voc + 6) % N_VOCAB),
        }
        ctx_peers = [((ctx + i) % N_CTX, voc) for i in range(1, N_CTX)]
        voc_peers = [(ctx, (voc + i) % N_VOCAB) for i in range(1, N_VOCAB)]
        cross = (at(x, 1 - zl, core), y * 2 + 1 - zh)
        barrier = pltpu.get_barrier_semaphore()
        greeted = ctx_peers + voc_peers + [cross]
        for peer in greeted:
            pl.semaphore_signal(barrier, inc=1, device_id=peer, device_id_type=MESH)

        def own_rows(phase, which):
            return pl.ds(pl.multiple_of(at(x, zl, which) * toks[phase], 16), toks[phase])

        def load(phase):
            return pltpu.make_async_copy(
                hid_hbm.at[pl.ds(offs[phase], toks[phase]), :], H[phase].at[own_rows(phase, core), :],
                hid_sem.at[phase])

        for phase in range(n_phase):
            load(phase).start()
        w_load = pltpu.make_async_copy(w_hbm, W, w_sem)
        LB[ctx] = lab_ref[...]
        xs = {"0": x, "L": left, "R": right, "2": across}

        def region_at(phase, region, which):
            ahead = starts[phase][region]
            back = half - ahead - cols[phase][region]
            return pl.multiple_of(which * half + jnp.where(q == 0, ahead, back), LANES)

        def piece(key):
            phase, block, region, part = key
            xb = xs[block[-1]]
            zb = 1 - zl if block[0] == "Z" else zl
            row = at(xb, zb, 1 - core if part else core) * toks[phase]
            return H[phase].at[
                pl.ds(pl.multiple_of(row, 16), toks[phase]),
                pl.ds(region_at(phase, region, core), cols[phase][region])]

        def link_copy(link, key):
            ref = piece(key)
            return remote(ref, ref, send.at[key[0], LINKS.index(link)], recv.at[sem_of[landing(link, key)]],
                          device[link])

        def take(key):
            ref = piece(key)
            phase, block, region, _ = key
            remote(ref, ref, send.at[phase, 6], recv.at[sem_of[key]], pair).wait_recv()
            remote(ref, ref, send.at[phase, 6], pair_recv.at[group_of[(phase, block[-1], region)]], pair).start()

        def drain(phase, a, b, sem):
            ref = H[phase].at[pl.ds(0, a), pl.ds(0, b)]
            return remote(ref, ref, sem, sem, pair)

        def own_copy(phase, theirs):
            first = pl.multiple_of((1 - core if theirs else core) * half, LANES)
            ref = H[phase].at[own_rows(phase, core), pl.ds(first, half)]
            return remote(ref, ref, own_send.at[phase], (own_recv if theirs else rest_recv).at[phase], pair)

        def stat_copy(buf, phase, index, stage, peer):
            ref = buf[phase].at[index]
            return remote(ref, ref, st_send.at[phase, stage], st_recv.at[phase, stage], peer)

        def stat_all(buf, phase, stage, n):
            ref = buf[phase].at[pl.ds(0, n - 1)]
            return remote(ref, ref, st_send.at[phase, stage], st_recv.at[phase, stage], pair)

        def label_all():
            ref = LB.at[pl.ds(0, N_CTX - 1)]
            return remote(ref, ref, lb_send, lb_recv, pair)

        for phase in range(n_phase):
            load(phase).wait()
        w_load.start()
        pl.semaphore_wait(barrier, len(greeted))
        for phase in range(n_phase):
            own_copy(phase, True).start()
            own_copy(phase, False).start()

        first_col = (ctx * N_VOCAB + voc) * n_cols
        seen = set()

        def once(*what):
            new = what not in seen
            seen.add(what)
            return new

        def block_rows(phase, xb):
            n = 4 * toks[phase]
            return pl.ds(pl.multiple_of(xb * n, n), n)

        def logits_task(phase, region, tile):
            if once("w"):
                w_load.wait()
            for b in tile:
                if once("group", phase, b, region):
                    n = toks[phase] * (2 if b == "0" else 4)
                    drain(phase, n, cols[phase][region], pair_recv.at[group_of[(phase, b, region)]]).wait_recv()
                if b == "0" and once("rest", phase):
                    drain(phase, toks[phase], half, rest_recv.at[phase]).wait_recv()
            spans = [pl.ds(region_at(phase, region, which), cols[phase][region]) for which in (core, 1 - core)]
            left_side = jnp.concatenate([W[k, :] for k in spans], axis=0)

            def product(blocks):
                rows = [block_rows(phase, xb) for xb in blocks]
                right_side = jnp.concatenate(
                    [jnp.concatenate([H[phase][r, k] for k in spans], axis=1) for r in rows], axis=0)
                part = lax.dot_general(
                    left_side, right_side, (((0,), (1,)), ((), ())), preferred_element_type=jnp.float32)
                for i, xb in enumerate(blocks):
                    piece_of = part[:, i * width[phase]:(i + 1) * width[phase]]
                    if region == REGIONS[0]:
                        LT[phase][xb] = piece_of
                    else:
                        LT[phase][xb] += piece_of

            if toks[phase] == 64:
                first = BLOCKS.index(tile[0])
                pl.loop(first, first + 2)(lambda i: product([lax.rem(x + i, N_X)]))
            else:
                product([xs[b] for b in tile])

        def label_mask(phase, i):
            ids = lax.broadcasted_iota(jnp.int32, (n_cols, width[phase]), 0)
            return ids == LR[phase][i] - first_col

        def label_rows():
            label_all().wait_recv()
            for phase, tok in enumerate(toks):
                per = width[phase] // tok
                for i in range(n_block[phase]):
                    LR[phase][i] = jnp.concatenate(
                        [LB[i * per + j][:, offs[phase]:offs[phase] + tok] for j in range(per)], axis=1)

        def stats_task(phase):
            if once("labels"):
                label_rows()
            per = width[phase] // LANES
            for i in range(n_block[phase]):
                lt = LT[phase][i]
                top = jnp.max(lt, axis=0, keepdims=True)
                total = jnp.sum(jnp.exp(lt - top), axis=0, keepdims=True)
                label = jnp.sum(jnp.where(label_mask(phase, i), lt, 0.0), axis=0, keepdims=True)
                for k, row in enumerate((top, total, label)):
                    for j in range(per):
                        r = i * per + j
                        S1[phase][ctx, k, r:r + 1, :] = row[:, j * LANES:(j + 1) * LANES]
            for peer in ctx_peers:
                stat_copy(S1, phase, ctx, 0, peer).start()

        def merged(buf, n):
            tops = [buf[i, 0] for i in range(n)]
            top = tops[0]
            for t in tops[1:]:
                top = jnp.maximum(top, t)
            total = sum(buf[i, 1] * jnp.exp(tops[i] - top) for i in range(n))
            return top, total, sum(buf[i, 2] for i in range(n))

        def merge1_task(phase):
            stat_all(S1, phase, 0, N_CTX).wait_recv()
            for k, row in enumerate(merged(S1[phase], N_CTX)):
                S2[phase][voc, k] = row
            for peer in voc_peers:
                stat_copy(S2, phase, voc, 1, peer).start()

        def merge2_task(phase):
            stat_all(S2, phase, 1, N_VOCAB).wait_recv()
            top, total, label = merged(S2[phase], N_VOCAB)
            lp = top + jnp.log(total)
            LP[phase][0] = lp
            LP[phase][1] = lp - label + z_weight * lp * lp
            first = ctx * toks[phase]
            row = LP[phase][1, pl.ds(first // LANES, 1), :]
            row = pltpu.roll(row, (offs[phase] - first % LANES + LANES) % LANES, 1)
            lane = lax.broadcasted_iota(jnp.int32, (1, LANES), 1)
            mine = (lane >= offs[phase]) & (lane < offs[phase] + toks[phase])
            loss[...] = jnp.where(mine, row, loss[...])

        def slope_task(phase):
            per = width[phase] // LANES
            for i in range(n_block[phase]):
                lp = jnp.concatenate([LP[phase][0, i * per + j:i * per + j + 1, :] for j in range(per)], axis=1)
                soft = jnp.exp(LT[phase][i] - lp)
                hot = jnp.where(label_mask(phase, i), 1.0, 0.0)
                ST[phase][:, i * width[phase]:(i + 1) * width[phase]] = (
                    (1.0 + 2.0 * z_weight * lp) * soft - hot).astype(jnp.bfloat16)

        def grad_run(phase, first, last):
            if first == last:
                grad_task(phase, first)
            else:
                pl.loop(first, last + 1)(lambda i: grad_task(phase, i))

        def grad_task(phase, i):
            rs = pl.ds(i * grad_step if isinstance(i, int) else pl.multiple_of(i * grad_step, grad_step), grad_step)
            part = lax.dot_general(
                H[phase][:, rs], ST[phase][...], (((0,), (1,)), ((), ())), preferred_element_type=jnp.float32)
            if phase == 0:
                grad[rs, :] = part
            else:
                grad[rs, :] += part

        run = {"logits": logits_task, "stats": stats_task, "merge1": merge1_task, "merge2": merge2_task,
               "slope": slope_task, "grad": grad_run}
        loss[...] = jnp.zeros_like(loss)
        for step in steps:
            if step[0] == "send":
                link_copy(step[1], step[2]).start()
            elif step[0] == "take":
                take(step[1])
            elif step[0] == "own":
                drain(step[1], toks[step[1]], half, own_recv.at[step[1]]).wait_recv()
                if step[1] == 0:
                    for peer in ctx_peers:
                        remote(LB.at[ctx], LB.at[ctx], lb_send, lb_recv, peer).start()
            else:
                run[step[1][0]](*step[1][1:])

        for phase in range(n_phase):
            for i, link in enumerate(LINKS):
                total = sum(cols[phase][s[2][2]] // unit for s in steps
                            if s[0] == "send" and s[1] == link and s[2][0] == phase)
                a, b = rectangle(total, N_CTX, depth // unit)
                drain(phase, a * toks[phase], b * unit, send.at[phase, i]).wait_send()
            drain(phase, 14 * toks[phase], half, send.at[phase, 6]).wait_send()
            drain(phase, toks[phase], depth, own_send.at[phase]).wait_send()
            stat_all(S1, phase, 0, N_CTX).wait_send()
            stat_all(S2, phase, 1, N_VOCAB).wait_send()
        label_all().wait_send()

    bf16, f32, i32 = jnp.bfloat16, jnp.float32, jnp.int32
    dma = pltpu.SemaphoreType.DMA
    vmem = pl.BlockSpec(memory_space=pltpu.VMEM)
    tokens = [N_CTX * t for t in toks]
    return pl.pallas_call(
        kernel,
        name="gather_head",
        out_shape=(pltpu.VMEM((depth, n_cols), f32), pltpu.VMEM((tokens[-1], depth), bf16),
                   pltpu.VMEM((n_cols, tokens[-1]), bf16), pltpu.VMEM((1, LANES), f32)),
        in_specs=[pl.BlockSpec(memory_space=pl.ANY), vmem, pl.BlockSpec(memory_space=pl.ANY)],
        out_specs=(vmem,) * 4,
        scratch_shapes=[
            *(pltpu.VMEM((n, depth), bf16) for n in tokens[:-1]),
            *(pltpu.VMEM((n_cols, n), bf16) for n in tokens[:-1]),
            *(pltpu.VMEM((n, n_cols, w), f32) for n, w in zip(n_block, width)),
            *(pltpu.VMEM((N_CTX, 3, n, LANES), f32) for n in n_row),
            *(pltpu.VMEM((N_VOCAB, 3, n, LANES), f32) for n in n_row),
            *(pltpu.VMEM((2, n, LANES), f32) for n in n_row),
            *(pltpu.VMEM((n, 1, w), i32) for n, w in zip(n_block, width)),
            pltpu.VMEM((depth, n_cols), bf16),
            pltpu.VMEM((N_CTX, 1, LANES), i32),
            dma((n_phase,)), dma, dma((len(keys),)), dma((len(groups),)), dma((n_phase,)), dma((n_phase,)),
            dma((n_phase, 7)), dma((n_phase,)), dma((n_phase, 2)), dma((n_phase, 2)), dma, dma,
        ],
        compiler_params=pltpu.CompilerParams(
            collective_id=0, has_side_effects=True, vmem_limit_bytes=42 * 2**20),
    )(hidden, labels.reshape(1, LANES), head_weight)


def finish(grad, h_last, st_last, loss):
    depth, n_cols = grad.shape
    step, slots = 1024, 3
    n = depth // step

    def kernel(grad_ref, h_ref, st_ref, loss_ref, out, loss_out, buf, sem):
        def copy(i):
            k = lax.rem(i, slots)
            return pltpu.make_async_copy(
                buf.at[k], out.at[pl.ds(pl.multiple_of(i * step, step), step), :], sem.at[k])

        loss_out[...] = loss_ref[...]

        @pl.loop(0, n)
        def _(i):
            @pl.when(i >= slots)
            def _():
                copy(i).wait()

            rs = pl.ds(pl.multiple_of(i * step, step), step)
            buf[lax.rem(i, slots)] = grad_ref[rs, :] + lax.dot_general(
                h_ref[:, rs], st_ref[...], (((0,), (1,)), ((), ())), preferred_element_type=jnp.float32)
            copy(i).start()

        for i in range(max(0, n - slots), n):
            copy(i).wait()

    vmem = pl.BlockSpec(memory_space=pltpu.VMEM)
    return pl.pallas_call(
        kernel,
        name="finish",
        out_shape=(jax.ShapeDtypeStruct((depth, n_cols), jnp.float32), jax.ShapeDtypeStruct((1, LANES), jnp.float32)),
        in_specs=[vmem] * 4,
        out_specs=(pl.BlockSpec(memory_space=pl.ANY), vmem),
        scratch_shapes=[pltpu.VMEM((slots, step, n_cols), jnp.float32), pltpu.SemaphoreType.DMA((slots,))],
        compiler_params=pltpu.CompilerParams(vmem_limit_bytes=16 * 2**20),
    )(grad, h_last, st_last, loss)


def head(hidden, labels, head_weight):
    parts = gather_head(hidden, labels, head_weight)
    parts = [pltpu.with_memory_space_constraint(p, pltpu.VMEM) for p in parts]
    grad, loss = finish(*parts)
    return loss.reshape(labels.shape), grad


def solution(mesh):
    return jax.shard_map(
        head,
        mesh=mesh,
        in_specs=(P("ctx", None), P("ctx"), P(None, ("ctx", "vocab"))),
        out_specs=(P("ctx"), P(None, ("ctx", "vocab"))),
        check_vma=False,
    )
```
